256 devices in a mesh: group: 8 (over z_lo, y), dev: 32 (over x, z_hi, core).
Axes of the slice: x: 4, y: 4, z: 8 (z_hi: 4, z_lo: 2; z = z_hi * 2 + z_lo), core: 2. Of those that a mesh axis runs over, the one named last changes fastest.
Arguments:
- stored_q: float32 [8, 192, 8192], P('group', 'dev'), may hold values from -1.75 to 1.75
- stored_kv: float32 [8, 64, 16384], P('group', 'dev'), may hold values from -1.75 to 1.75
- stored_o: float32 [8, 448, 8192], P('group', 'dev'), may hold values from -1.75 to 1.75
- owner_map: int32 [32, 8], replicated, may hold values from 0 to 7, each once within a row
Outputs:
- q_fold: bfloat16 [64, 1536, 512], P('dev')
- o_fold: bfloat16 [64, 512, 3584], P('dev')
The draws below stay inside these ranges and needn't reach their ends.
Inputs may be any that keep to these rules, and one draw needn't show every extreme that they name: Each row of owner_map names every trainer slot once.
All inputs are finite; a program needn't handle non-finite values.
Results may differ from the reference program's by a relative error of at most 0.001.
Values may be sent and summed in bfloat16 or wider, within the bound.
A program may use at most 128 MiB of HBM per device.

```python
import jax
import jax.numpy as jnp
from jax import lax

H = 64
HD = 128
QR = 1536
KVL = 512
DW = 3584
SLOTS = 8
SEGMENTS = 32


def level_of(rng, extent, split, least, top_value):
    loudness = 1.0
    for axis_at, blocks in split:
        steps = jax.random.uniform(jax.random.fold_in(jax.random.fold_in(rng, 6), axis_at), (blocks,), jnp.float32, least / len(split), top_value / len(split))
        loudness = loudness * jnp.repeat(jnp.exp(steps), extent[axis_at] // blocks).reshape((-1,) + (1,) * (len(extent) - 1 - axis_at))
    return loudness


def gaussian(stream_key, shape, width, bound, pieces=(), dtype=jnp.bfloat16):
    factor_of = level_of(stream_key, shape, pieces, -0.22, 0.18) if pieces else 1.0
    entries = jax.random.normal(stream_key, shape, jnp.float32) * width * factor_of
    return jnp.minimum(jnp.maximum(entries, -bound), bound).astype(dtype)


def setup_inputs(seed: int = 0) -> dict:
    splits = jax.random.split(jax.random.key(seed), 5)
    stored_q = gaussian(splits[0], (SLOTS, QR // SLOTS, H * HD), 0.3, 1.75, ((0, 8), (1, 32)), jnp.float32)
    stored_kv = gaussian(splits[1], (SLOTS, KVL // SLOTS, 2 * H * HD), 0.3, 1.75, ((0, 8), (1, 32)), jnp.float32)
    stored_o = gaussian(splits[2], (SLOTS, DW // SLOTS, H * HD), 0.3, 1.75, ((0, 8), (1, 32)), jnp.float32)
    owner_map = jax.vmap(lambda own: jax.random.permutation(own, SLOTS))(jax.random.split(splits[3], SEGMENTS)).reshape((SEGMENTS, SLOTS)).astype(jnp.int32)
    return dict(stored_q=stored_q, stored_kv=stored_kv, stored_o=stored_o, owner_map=owner_map)


def reorder(values, owner_map, axis_pos):
    seg_count, slot_count = owner_map.shape
    full_shape = values.shape
    per_piece = full_shape[axis_pos] // (slot_count * seg_count)
    inner = full_shape[:axis_pos] + (slot_count, seg_count, per_piece) + full_shape[axis_pos + 1:]
    grouped = values.reshape(inner)
    tail = len(full_shape) - axis_pos - 1
    slot_index = owner_map.T.astype(jnp.int32).reshape((1,) * axis_pos + (slot_count, seg_count, 1) + (1,) * tail)
    slot_index = jnp.broadcast_to(slot_index, inner)
    picked = jnp.take_along_axis(grouped, slot_index, axis=axis_pos)
    picked = jnp.swapaxes(picked, axis_pos, axis_pos + 1)
    return picked.reshape(full_shape)


def fold_heads(query_rows, latent, output):
    heads = query_rows.shape[1] // HD
    query3 = query_rows.reshape(query_rows.shape[0], heads, HD).astype(jnp.float32)
    latent4 = latent.reshape(latent.shape[0], heads, 2, HD).astype(jnp.float32)
    out3 = output.reshape(output.shape[0], heads, HD).astype(jnp.float32)
    q_part = jnp.einsum("rhe,che->hrc", query3, latent4[:, :, 0], precision=lax.Precision.HIGHEST)
    o_part = jnp.einsum("che,whe->hcw", latent4[:, :, 1], out3, precision=lax.Precision.HIGHEST)
    return q_part.astype(jnp.bfloat16), o_part.astype(jnp.bfloat16)


def reference(stored_q, stored_kv, stored_o, owner_map):
    q_up = reorder(stored_q.reshape(-1, stored_q.shape[2]), owner_map, 0)
    kv_up = reorder(stored_kv.reshape(-1, stored_kv.shape[2]), owner_map, 0)
    o_proj = reorder(stored_o.reshape(-1, stored_o.shape[2]), owner_map, 0)
    q_fold, o_fold = fold_heads(q_up, kv_up, o_proj)
    return (q_fold, o_fold)
```

```python
import jax
import jax.numpy as jnp
from jax import lax
from jax.experimental import pallas as pl
from jax.experimental.pallas import tpu as pltpu
from jax.sharding import PartitionSpec as P

MESH = pl.DeviceIdType.MESH
F32, BF16, I32 = jnp.float32, jnp.bfloat16, jnp.int32
NG, ND = 8, 32
ROWS = 16
GROW = 1.008 / 32767.0
LEAST = 2.0**-120


def nt(a, b):
    return lax.dot_general(a, b, (((1,), (1,)), ((), ())), preferred_element_type=F32)


def kernel(q_ref, kv_ref, o_ref, own_ref, qf_ref, of_ref,
           send, ssend, gat, gsc, sca, jmap, inv, qm, km, om, vm,
           a_send, a_recv, s_send, s_recv):
    g = lax.axis_index("group")
    d = lax.axis_index("dev")
    zl, y = g // 4, g % 4
    up, down, far = (y + 1) % 4, (y + 3) % 4, (y + 2) % 4
    mine, other = zl * 4, (1 - zl) * 4
    near = {"z": (other + y, d), "p": (mine + up, d), "m": (mine + down, d)}

    barrier = pltpu.get_barrier_semaphore()

    def greet(i, _):
        pl.semaphore_signal(barrier, inc=1, device_id=(g, (d + i) % ND), device_id_type=MESH)
        return 0

    lax.fori_loop(1, ND, greet, 0)
    for who in near.values():
        pl.semaphore_signal(barrier, inc=1, device_id=who, device_id_type=MESH)

    row = lax.broadcasted_iota(I32, (ROWS, 128), 0)
    lane = lax.broadcasted_iota(I32, (ROWS, 128), 1)

    def quantise(i, _):
        c0 = pl.multiple_of(i * 256, 256)
        c1 = pl.multiple_of(i * 512, 512)
        qs = [q_ref[0, :, pl.ds(c0 + 128 * h, 128)] for h in range(2)]
        os = [o_ref[0, :, pl.ds(c0 + 128 * h, 128)] for h in range(2)]
        ks = [kv_ref[0, :, pl.ds(c1 + 128 * h, 128)] for h in range(4)]
        blocks = (
            jnp.concatenate([qs[0], qs[1], ks[0], ks[2]], axis=0),
            jnp.concatenate([os[0], ks[1]], axis=0),
            jnp.concatenate([os[1], ks[3]], axis=0),
        )
        packed = jnp.zeros((1, 128), F32)
        for t, x in enumerate(blocks):
            top = jnp.max(jnp.abs(x), axis=1, keepdims=True)
            scale = jnp.maximum((top * GROW).astype(BF16).astype(F32), LEAST)
            code = jnp.round(x * (1.0 / scale)).astype(I32)
            send[t, i] = code.astype(jnp.int16)
            spread = jnp.where(lane == row + ROWS * t, scale, 0.0)
            packed = packed + jnp.sum(spread, axis=0, keepdims=True)
        ssend[i] = packed
        return 0

    lax.fori_loop(0, ND, quantise, 0, unroll=2)
    pl.semaphore_wait(barrier, ND + 2)

    def out_of(t):
        return ssend if t == 3 else send.at[t]

    def into(t, group):
        return gsc.at[group] if t == 3 else gat.at[t, group]

    def exchange(t):
        src, dst = out_of(t), into(t, g)

        def one(i, _):
            to = (d + i) % ND
            pltpu.make_async_remote_copy(
                src_ref=src.at[to], dst_ref=dst.at[d], send_sem=a_send.at[t], recv_sem=a_recv.at[t],
                device_id=(g, to), device_id_type=MESH).start()
            return 0

        lax.fori_loop(1, ND, one, 0)
        if t == 3:
            gsc[g, d] = ssend[d]
        else:
            gat[t, g, d] = send[t, d]

    for t in (0, 3, 1, 2):
        exchange(t)

    r = lax.broadcasted_iota(I32, (128, 128), 0)
    k = lax.broadcasted_iota(I32, (128, 128), 1)
    kin = k - (k // ROWS) * ROWS

    def piece(rem, size):
        return sum(((rem >= size * n).astype(I32) for n in range(1, NG)), jnp.zeros_like(rem))

    h1 = (r >= 48).astype(I32)
    rq = r - 48 * h1
    jq = piece(rq, 6)
    h2 = (r >= 112).astype(I32)
    rk = r - 96 - 16 * h2
    jk = piece(rk, 2)
    offset = jnp.where(r < 96, rq - 6 * jq + 6 * h1, rk - 2 * jk + 12 + 2 * h2)
    jmap[0] = jnp.where(offset == kin, jnp.where(r < 96, jq, jk), -1)
    jo = piece(r, 14)
    rv = r - 112
    jv = piece(rv, 2)
    offset = jnp.where(r < 112, r - 14 * jo, rv - 2 * jv + 14)
    jmap[1] = jnp.where(offset == kin, jnp.where(r < 112, jo, jv), -1)
    kg = lax.broadcasted_iota(I32, (ND, 128), 1) // ROWS
    held = jnp.zeros((ND, 128), I32)
    for j in range(NG):
        held = held + jnp.where(own_ref[:, j:j + 1] == kg, j, 0)
    inv[...] = held

    def hop(t, kind, ref, who):
        n = t * 9 + kind
        return pltpu.make_async_remote_copy(
            src_ref=ref, dst_ref=ref, send_sem=s_send.at[n], recv_sem=s_recv.at[n],
            device_id=who, device_id_type=MESH)

    started = []

    def go(*args):
        c = hop(*args)
        c.start()
        started.append(c)

    def half(t, group, n):
        return into(t, group).at[pl.ds(n * (ND // 2), ND // 2)]

    def own(t):
        whole = into(t, g).at[pl.ds(0, ND - 1)]
        pltpu.make_async_copy(whole, whole, a_recv.at[t]).wait()
        go(t, 0, into(t, g), near["z"])
        go(t, 1, into(t, g), near["p"])
        go(t, 2, into(t, g), near["m"])

    def partner(t):
        ref = into(t, other + y)
        hop(t, 0, ref, near["z"]).wait_recv()
        go(t, 3, ref, near["p"])
        go(t, 4, ref, near["m"])

    def forward(t, b):
        base = (mine, other)[b]
        hop(t, 1 + 2 * b, into(t, base + down), near["p"]).wait_recv()
        go(t, 5 + 2 * b, half(t, base + down, 0), near["p"])
        hop(t, 2 + 2 * b, into(t, base + up), near["m"]).wait_recv()
        go(t, 6 + 2 * b, half(t, base + up, 1), near["m"])

    def finish(t):
        for b, base in enumerate((mine, other)):
            hop(t, 5 + 2 * b, half(t, base + far, 0), near["p"]).wait_recv()
            hop(t, 6 + 2 * b, half(t, base + far, 1), near["m"]).wait_recv()

    def scales():
        at = lax.broadcasted_iota(I32, (1, 128), 1) // ROWS

        def one(i, _):
            for t in range(3):
                line = jnp.zeros((1, 128), F32)
                for n in range(NG):
                    line = line + jnp.where(at == n, pltpu.roll(gsc[n, i], (ROWS * (n - t)) % 128, 1), 0.0)
                sca[t, i] = line
            return 0

        lax.fori_loop(0, ND, one, 0)

    def decode(t, i):
        code = gat[t, :, i].reshape(128, 128).astype(F32)
        hi = code.astype(BF16)
        lo = (code - hi.astype(F32)).astype(BF16)
        pick = jnp.where(jmap[min(t, 1)] == inv[pl.ds(i, 1), :], sca[t, i], 0.0).astype(BF16)
        got = jnp.dot(pick, jnp.concatenate([hi, lo], axis=1), preferred_element_type=F32)
        x = got[:, :128] + got[:, 128:]
        hi = x.astype(BF16)
        return hi, (x - hi.astype(F32)).astype(BF16)

    def queries():
        def one(i, _):
            hi, lo = decode(0, i)
            at = pl.ds(pl.multiple_of(i * 48, 16), 48)
            kat = pl.ds(pl.multiple_of(i * 16, 16), 16)
            for h in range(2):
                qm[h, at, 0:128] = hi[48 * h:48 * h + 48]
                qm[h, at, 128:256] = lo[48 * h:48 * h + 48]
                s = slice(96 + 16 * h, 112 + 16 * h)
                km[h, kat, 0:128] = hi[s]
                km[h, kat, 128:256] = hi[s]
                km[h, kat, 256:384] = lo[s]
            return 0

        lax.fori_loop(0, ND, one, 0)
        for h in range(2):
            def tile(i, _):
                at = pl.ds(pl.multiple_of(i * 256, 256), 256)
                x = nt(qm[h, at, :], km[h, :, 0:256]) + nt(qm[h, at, 0:128], km[h, :, 256:384])
                qf_ref[h, at, :] = x.astype(BF16)
                return 0

            lax.fori_loop(0, 6, tile, 0)

    def outputs(h):
        def one(i, _):
            hi, lo = decode(1 + h, i)
            at = pl.ds(pl.multiple_of(i * 112, 16), 112)
            vat = pl.ds(pl.multiple_of(i * 16, 16), 16)
            om[at, 0:128] = hi[:112]
            om[at, 128:256] = hi[:112]
            om[at, 256:384] = lo[:112]
            vm[vat, 0:128] = hi[112:]
            vm[vat, 128:256] = lo[112:]
            return 0

        lax.fori_loop(0, ND, one, 0)

        def tile(i, _):
            at = pl.ds(pl.multiple_of(i * 256, 256), 256)
            x = nt(vm[...], om[at, 0:256]) + nt(vm[:, 0:128], om[at, 256:384])
            of_ref[h, :, at] = x.astype(BF16)
            return 0

        lax.fori_loop(0, 14, tile, 0)

    own(0)
    own(3)
    own(1)
    partner(0)
    partner(3)
    own(2)
    forward(0, 0)
    forward(3, 0)
    partner(1)
    forward(0, 1)
    forward(3, 1)
    partner(2)
    forward(1, 0)
    finish(0)
    finish(3)
    scales()
    queries()
    forward(1, 1)
    forward(2, 0)
    finish(1)
    outputs(0)
    forward(2, 1)
    finish(2)
    outputs(1)
    for c in started:
        c.wait_send()
    for t in range(4):
        sent = out_of(t).at[pl.ds(0, ND - 1)]
        pltpu.make_async_copy(sent, sent, a_send.at[t]).wait()


def body(stored_q, stored_kv, stored_o, owner_map):
    vmem = pl.BlockSpec(memory_space=pltpu.VMEM)
    return pl.pallas_call(
        kernel,
        out_shape=(pltpu.VMEM((2, 1536, 512), BF16), pltpu.VMEM((2, 512, 3584), BF16)),
        in_specs=[vmem] * 4,
        out_specs=(vmem, vmem),
        scratch_shapes=[
            pltpu.VMEM((3, ND, ROWS, 128), jnp.int16),
            pltpu.VMEM((ND, 1, 128), F32),
            pltpu.VMEM((3, NG, ND, ROWS, 128), jnp.int16),
            pltpu.VMEM((NG, ND, 1, 128), F32),
            pltpu.VMEM((3, ND, 1, 128), F32),
            pltpu.VMEM((2, 128, 128), I32),
            pltpu.VMEM((ND, 128), I32),
            pltpu.VMEM((2, 1536, 256), BF16),
            pltpu.VMEM((2, 512, 384), BF16),
            pltpu.VMEM((3584, 384), BF16),
            pltpu.VMEM((512, 256), BF16),
            pltpu.SemaphoreType.DMA((4,)),
            pltpu.SemaphoreType.DMA((4,)),
            pltpu.SemaphoreType.DMA((36,)),
            pltpu.SemaphoreType.DMA((36,)),
        ],
        compiler_params=pltpu.CompilerParams(
            collective_id=0, has_side_effects=True, vmem_limit_bytes=40 * 1024 * 1024),
    )(stored_q, stored_kv, stored_o, owner_map)


def solution(mesh):
    in_specs = (P("group", "dev", None), P("group", "dev", None), P("group", "dev", None), P())
    out_specs = (P("dev", None, None), P("dev", None, None))
    return jax.shard_map(body, mesh=mesh, in_specs=in_specs, out_specs=out_specs, check_vma=False)
```

```python
import jax
import jax.numpy as jnp
from jax import lax
from jax.experimental import pallas as pl
from jax.experimental.pallas import tpu as pltpu
from jax.sharding import PartitionSpec as P

MESH = pl.DeviceIdType.MESH
F32, BF16, I32 = jnp.float32, jnp.bfloat16, jnp.int32
NG, ND = 8, 32
ROWS = 16
NEAR, FAR = 8, 24
GROW = 1.008 / 32767.0
LEAST = 2.0**-120


def nt(a, b):
    return lax.dot_general(a, b, (((1,), (1,)), ((), ())), preferred_element_type=F32)


def fold_out(v, o):
    return (nt(v[:, 0:256], o[:, 0:256]) + nt(v[:, 0:128], o[:, 256:384])).astype(BF16)


def kernel(q_hbm, kv_hbm, o_hbm, own_ref, qf_ref, of_ref, om1, vm1,
           q_ref, kv_ref, o_ref, near, nsc, send, ssend, gat, gsc, sca, jmap, inv, qm, km, om0, vm0,
           in_sem, a_send, a_recv, x_send, x_recv, s_send, s_recv):
    loads = [pltpu.make_async_copy(a, b, in_sem.at[n])
             for n, (a, b) in enumerate(((q_hbm, q_ref), (kv_hbm, kv_ref), (o_hbm, o_ref)))]
    for c in loads:
        c.start()
    g = lax.axis_index("group")
    d = lax.axis_index("dev")
    zl, y = g // 4, g % 4
    zh, xc = (d // 2) % 4, (d // 8) * 2 + d % 2
    up, down, far = (y + 1) % 4, (y + 3) % 4, (y + 2) % 4
    mine, other = zl * 4, (1 - zl) * 4
    to_z, to_p, to_m = (other + y, d), (mine + up, d), (mine + down, d)

    def dev_at(z, n):
        return ((n // 2) * 4 + z) * 2 + n % 2

    barrier = pltpu.get_barrier_semaphore()

    def greet(i, _):
        pl.semaphore_signal(barrier, inc=1, device_id=(g, (d + i) % ND), device_id_type=MESH)
        return 0

    lax.fori_loop(1, ND, greet, 0)
    for who in (to_z, to_p, to_m):
        pl.semaphore_signal(barrier, inc=1, device_id=who, device_id_type=MESH)

    row = lax.broadcasted_iota(I32, (ROWS, 128), 0)
    lane = lax.broadcasted_iota(I32, (ROWS, 128), 1)

    def quantise(i):
        qs = [q_ref[:, 2 * i + h, :] for h in range(2)]
        os = [o_ref[:, 2 * i + h, :] for h in range(2)]
        ks = [kv_ref[i, 2 * h:2 * h + 2, :] for h in range(4)]
        blocks = (
            jnp.concatenate([qs[0], qs[1], ks[0], ks[2]], axis=0),
            jnp.concatenate([os[0], ks[1]], axis=0),
            jnp.concatenate([os[1], ks[3]], axis=0),
        )
        codes, packed = [], jnp.zeros((1, 128), F32)
        for t, x in enumerate(blocks):
            top = jnp.max(jnp.abs(x), axis=1, keepdims=True)
            scale = jnp.maximum((top * GROW).astype(BF16).astype(F32), LEAST)
            codes.append(jnp.round(x * (1.0 / scale)).astype(I32).astype(jnp.int16))
            spread = jnp.where(lane == row + ROWS * ((t + g) % NG), scale, 0.0)
            packed = packed + jnp.sum(spread, axis=0, keepdims=True)
        return codes, packed

    def code_near(n, _):
        codes, packed = quantise(dev_at(zh, n))
        for t in range(3):
            near[t, g, n] = codes[t]
        nsc[g, n] = packed
        return 0

    def code_far(n, _):
        codes, packed = quantise(dev_at((zh + 1 + n // NEAR) % 4, n % NEAR))
        for t in range(3):
            send[t, n] = codes[t]
        ssend[n] = packed
        return 0

    for c in loads:
        c.wait()
    lax.fori_loop(0, NEAR, code_near, 0, unroll=2)
    lax.fori_loop(0, FAR, code_far, 0, unroll=2)
    pl.semaphore_wait(barrier, ND + 2)

    def into(part, group):
        if part < 4:
            return nsc.at[group] if part == 3 else near.at[part, group]
        ref = gsc.at[group] if part == 7 else gat.at[part - 4, group]
        return ref.at[pl.ds(NEAR, FAR)]

    def half(part, group, n):
        size = (NEAR if part < 4 else FAR) // 2
        return into(part, group).at[pl.ds(n * size, size)]

    def hop(part, kind, ref, who):
        n = part * 9 + kind
        return pltpu.make_async_remote_copy(
            src_ref=ref, dst_ref=ref, send_sem=s_send.at[n], recv_sem=s_recv.at[n],
            device_id=who, device_id_type=MESH)

    started = []

    def go(*args):
        c = hop(*args)
        c.start()
        started.append(c)

    def own(part):
        go(part, 0, into(part, g), to_z)
        go(part, 1, into(part, g), to_p)
        go(part, 2, into(part, g), to_m)

    def partner(part):
        ref = into(part, other + y)
        hop(part, 0, ref, to_z).wait_recv()
        go(part, 3, ref, to_p)
        go(part, 4, ref, to_m)

    def forward(part, b):
        base = (mine, other)[b]
        hop(part, 1 + 2 * b, into(part, base + down), to_p).wait_recv()
        go(part, 5 + 2 * b, half(part, base + down, 0), to_p)
        hop(part, 2 + 2 * b, into(part, base + up), to_m).wait_recv()
        go(part, 6 + 2 * b, half(part, base + up, 1), to_m)

    def finish(part):
        for b, base in enumerate((mine, other)):
            hop(part, 5 + 2 * b, half(part, base + far, 0), to_p).wait_recv()
            hop(part, 6 + 2 * b, half(part, base + far, 1), to_m).wait_recv()

    def far_out(t):
        src = ssend if t == 3 else send.at[t]
        dst = gsc.at[g] if t == 3 else gat.at[t, g]

        def one(k, _):
            rel, n = k // NEAR, (xc + k) % NEAR
            pltpu.make_async_remote_copy(
                src_ref=src.at[rel * NEAR + n], dst_ref=dst.at[NEAR + (2 - rel) * NEAR + xc],
                send_sem=a_send.at[t], recv_sem=a_recv.at[t],
                device_id=(g, dev_at((zh + 1 + rel) % 4, n)), device_id_type=MESH).start()
            return 0

        lax.fori_loop(0, FAR, one, 0)

    def far_in(t):
        whole = into(t + 4, g)
        pltpu.make_async_copy(whole, whole, a_recv.at[t]).wait()

    def near_out(t):
        src = nsc if t == 3 else near.at[t]
        dst = gsc if t == 3 else gat.at[t]

        def one(k, _):
            n = (xc + k) % NEAR
            pltpu.make_async_remote_copy(
                src_ref=src.at[:, n], dst_ref=dst.at[:, xc],
                send_sem=x_send.at[t], recv_sem=x_recv.at[t],
                device_id=(g, dev_at(zh, n)), device_id_type=MESH).start()
            return 0

        lax.fori_loop(1, NEAR, one, 0)
        for n in range(NG):
            if t == 3:
                gsc[n, xc] = nsc[n, xc]
            else:
                gat[t, n, xc] = near[t, n, xc]

    def near_in(t):
        whole = (gsc if t == 3 else gat.at[t]).at[:, pl.ds(0, NEAR - 1)]
        pltpu.make_async_copy(whole, whole, x_recv.at[t]).wait()

    def maps():
        r = lax.broadcasted_iota(I32, (128, 128), 0)
        k = lax.broadcasted_iota(I32, (128, 128), 1)
        kin = k - (k // ROWS) * ROWS

        def piece(rem, size):
            return sum(((rem >= size * n).astype(I32) for n in range(1, NG)), jnp.zeros_like(rem))

        h1 = (r >= 48).astype(I32)
        rq = r - 48 * h1
        jq = piece(rq, 6)
        h2 = (r >= 112).astype(I32)
        rk = r - 96 - 16 * h2
        jk = piece(rk, 2)
        offset = jnp.where(r < 96, rq - 6 * jq + 6 * h1, rk - 2 * jk + 12 + 2 * h2)
        jmap[0] = jnp.where(offset == kin, jnp.where(r < 96, jq, jk), -1)
        jo = piece(r, 14)
        rv = r - 112
        jv = piece(rv, 2)
        offset = jnp.where(r < 112, r - 14 * jo, rv - 2 * jv + 14)
        jmap[1] = jnp.where(offset == kin, jnp.where(r < 112, jo, jv), -1)
        kg = lax.broadcasted_iota(I32, (ND, 128), 1) // ROWS
        held = jnp.zeros((ND, 128), I32)
        owner = own_ref[...].T
        for j in range(NG):
            held = held + jnp.where(owner[:, j:j + 1] == kg, j, 0)
        inv[...] = held

    def scales():
        at = lax.broadcasted_iota(I32, (ND, 128), 1) // ROWS
        lines = [gsc[n].reshape(ND, 128) for n in range(NG)]
        for t in range(3):
            held = jnp.zeros((ND, 128), F32)
            for n in range(NG):
                held = held + jnp.where(at == (n + t) % NG, lines[n], 0.0)
            sca[t] = pltpu.roll(held, (128 - ROWS * t) % 128, 1)

    def decode(t, pos):
        i = dev_at((zh + pos // NEAR) % 4, pos % NEAR)
        code = gat[t, :, pos].reshape(128, 128).astype(F32)
        hi = code.astype(BF16)
        lo = (code - hi.astype(F32)).astype(BF16)
        pick = jnp.where(jmap[min(t, 1)] == inv[pl.ds(i, 1), :], sca[t, pl.ds(pos, 1), :], 0.0).astype(BF16)
        got = jnp.dot(pick, jnp.concatenate([hi, lo], axis=1), preferred_element_type=F32)
        x = got[:, :128] + got[:, 128:]
        hi = x.astype(BF16)
        return i, hi, (x - hi.astype(F32)).astype(BF16)

    def decode_q(first, last):
        def one(pos, _):
            i, hi, lo = decode(0, pos)
            at = pl.ds(pl.multiple_of(i * 48, 16), 48)
            kat = pl.ds(pl.multiple_of(i * 16, 16), 16)
            for h in range(2):
                qm[h, at, 0:128] = hi[48 * h:48 * h + 48]
                qm[h, at, 128:256] = lo[48 * h:48 * h + 48]
                s = slice(96 + 16 * h, 112 + 16 * h)
                km[h, kat, 0:128] = hi[s]
                km[h, kat, 128:256] = hi[s]
                km[h, kat, 256:384] = lo[s]
            return 0

        lax.fori_loop(first, last, one, 0, unroll=4)

    def fold_q(h):
        def tile(i, _):
            at = pl.ds(pl.multiple_of(i * 768, 256), 768)
            x = nt(qm[h, at, :], km[h, :, 0:256]) + nt(qm[h, at, 0:128], km[h, :, 256:384])
            qf_ref[h, at, :] = x.astype(BF16)
            return 0

        lax.fori_loop(0, 2, tile, 0)

    def decode_o(h, first, last):
        om, vm = ((om0, vm0), (om1, vm1))[h]

        def one(pos, _):
            i, hi, lo = decode(1 + h, pos)
            at = pl.ds(pl.multiple_of(i * 112, 16), 112)
            vat = pl.ds(pl.multiple_of(i * 16, 16), 16)
            om[at, 0:128] = hi[:112]
            om[at, 128:256] = hi[:112]
            om[at, 256:384] = lo[:112]
            vm[vat, 0:128] = hi[112:]
            vm[vat, 128:256] = lo[112:]
            return 0

        lax.fori_loop(first, last, one, 0, unroll=4)

    def fold_o(first, last):
        def tile(i, _):
            at = pl.ds(pl.multiple_of(i * 256, 256), 256)
            of_ref[:, at] = fold_out(vm0, om0.at[at])
            return 0

        lax.fori_loop(first, last, tile, 0, unroll=2)

    order = (0, 3, 1, 2)
    for t in order:
        own(t)
    for t in order:
        far_out(t)
    maps()
    for t in order:
        partner(t)
    far_in(0)
    own(4)
    far_in(3)
    own(7)
    for t in order:
        forward(t, 0)
    partner(4)
    partner(7)
    for t in order:
        forward(t, 1)
    far_in(1)
    own(5)
    forward(4, 0)
    forward(7, 0)
    for t in order:
        finish(t)
        near_out(t)
    partner(5)
    forward(4, 1)
    forward(7, 1)
    far_in(2)
    own(6)
    partner(6)
    finish(7)
    near_in(3)
    scales()
    near_in(0)
    decode_q(0, NEAR)
    near_in(1)
    decode_o(0, 0, NEAR)
    near_in(2)
    decode_o(1, 0, NEAR)
    forward(5, 0)
    finish(4)
    decode_q(NEAR, ND)
    forward(5, 1)
    fold_q(0)
    forward(6, 0)
    fold_q(1)
    finish(5)
    decode_o(0, NEAR, ND)
    forward(6, 1)
    fold_o(0, 14)
    finish(6)
    decode_o(1, NEAR, ND)
    for c in started:
        c.wait_send()
    for t in range(4):
        sent = ssend if t == 3 else send.at[t]
        pltpu.make_async_copy(sent, sent, a_send.at[t]).wait()
        sent = (nsc if t == 3 else near.at[t]).at[:, pl.ds(0, NEAR - 1)]
        pltpu.make_async_copy(sent, sent, x_send.at[t]).wait()


def last_kernel(qf_ref, of_ref, om, vm, q_out, o_out, held, sem):
    whole = (pltpu.make_async_copy(qf_ref, q_out, sem.at[0]), pltpu.make_async_copy(of_ref, o_out.at[0], sem.at[1]))
    for c in whole:
        c.start()

    def out(i):
        at = pl.ds(pl.multiple_of(i * 256, 256), 256)
        return at, pltpu.make_async_copy(held.at[:, at], o_out.at[1, :, at], sem.at[2 + i])

    def tile(i, _):
        at, c = out(i)
        held[:, at] = fold_out(vm, om.at[at])
        c.start()
        return 0

    lax.fori_loop(0, 14, tile, 0, unroll=2)

    def done(i, _):
        out(i)[1].wait()
        return 0

    lax.fori_loop(0, 14, done, 0)
    for c in whole:
        c.wait()


def body(stored_q, stored_kv, stored_o, owner_map):
    vmem = pl.BlockSpec(memory_space=pltpu.VMEM)
    hbm = pl.BlockSpec(memory_space=pltpu.HBM)
    dma = pltpu.SemaphoreType.DMA
    far_inputs = [pltpu.with_memory_space_constraint(x, pltpu.HBM) for x in (
        stored_q.reshape(6, 64, 128),
        stored_kv.reshape(2, ND, 4, 128).transpose(1, 2, 0, 3).reshape(ND, 8, 128),
        stored_o.reshape(14, 64, 128))]
    parts = pl.pallas_call(
        kernel,
        out_shape=(pltpu.VMEM((2, 1536, 512), BF16), pltpu.VMEM((512, 3584), BF16),
                   pltpu.VMEM((3584, 384), BF16), pltpu.VMEM((512, 256), BF16)),
        in_specs=[hbm] * 3 + [vmem],
        out_specs=[vmem] * 4,
        scratch_shapes=[
            pltpu.VMEM((6, 64, 128), F32),
            pltpu.VMEM((ND, 8, 128), F32),
            pltpu.VMEM((14, 64, 128), F32),
            pltpu.VMEM((3, NG, NEAR, ROWS, 128), jnp.int16),
            pltpu.VMEM((NG, NEAR, 1, 128), F32),
            pltpu.VMEM((3, FAR, ROWS, 128), jnp.int16),
            pltpu.VMEM((FAR, 1, 128), F32),
            pltpu.VMEM((3, NG, ND, ROWS, 128), jnp.int16),
            pltpu.VMEM((NG, ND, 1, 128), F32),
            pltpu.VMEM((3, ND, 128), F32),
            pltpu.VMEM((2, 128, 128), I32),
            pltpu.VMEM((ND, 128), I32),
            pltpu.VMEM((2, 1536, 256), BF16),
            pltpu.VMEM((2, 512, 384), BF16),
            pltpu.VMEM((3584, 384), BF16),
            pltpu.VMEM((512, 256), BF16),
            dma((3,)), dma((4,)), dma((4,)), dma((4,)), dma((4,)), dma((72,)), dma((72,)),
        ],
        compiler_params=pltpu.CompilerParams(
            collective_id=0, has_side_effects=True, vmem_limit_bytes=32 * 1024 * 1024),
    )(*far_inputs, owner_map.T)
    return pl.pallas_call(
        last_kernel,
        out_shape=(jax.ShapeDtypeStruct((2, 1536, 512), BF16), jax.ShapeDtypeStruct((2, 512, 3584), BF16)),
        in_specs=[vmem] * 4,
        out_specs=[hbm] * 2,
        scratch_shapes=[pltpu.VMEM((512, 3584), BF16), dma((16,))],
        compiler_params=pltpu.CompilerParams(vmem_limit_bytes=32 * 1024 * 1024),
    )(*parts)


def solution(mesh):
    in_specs = (P("group", "dev", None), P("group", "dev", None), P("group", "dev", None), P())
    out_specs = (P("dev", None, None), P("dev", None, None))
    return jax.shard_map(body, mesh=mesh, in_specs=in_specs, out_specs=out_specs, check_vma=False)
```

```python
import jax
import jax.numpy as jnp
from jax import lax
from jax.experimental import pallas as pl
from jax.experimental.pallas import tpu as pltpu
from jax.sharding import PartitionSpec as P

MESH = pl.DeviceIdType.MESH
F32, BF16, I32 = jnp.float32, jnp.bfloat16, jnp.int32
NG, ND = 8, 32
ROWS = 16
NEAR, FAR = 8, 24
GROW = 1.008 / 32767.0
LEAST = 2.0**-120


def nt(a, b):
    return lax.dot_general(a, b, (((1,), (1,)), ((), ())), preferred_element_type=F32)


def fold(a, b):
    hi = b[:, 0:128]
    return (nt(a, jnp.concatenate([hi, hi], axis=1)) + nt(a[:, 0:128], b[:, 128:256])).astype(BF16)


def kernel(q_hbm, kv_hbm, o_hbm, own_hbm, qf_ref, of_ref, om1, vm1,
           q_ref, kv_ref, o_ref, own_ref, near, nsc, send, ssend, gat, gsc, sca, jmap, inv, qm, km, om0, vm0,
           in_sem, a_send, a_recv, x_send, x_recv, s_send, s_recv):
    loads = [pltpu.make_async_copy(a, b, in_sem.at[n])
             for n, (a, b) in enumerate(((q_hbm, q_ref), (kv_hbm, kv_ref), (o_hbm, o_ref), (own_hbm, own_ref)))]
    for c in loads:
        c.start()
    g = lax.axis_index("group")
    d = lax.axis_index("dev")
    zl, y = g // 4, g % 4
    zh, xc = (d // 2) % 4, (d // 8) * 2 + d % 2
    up, down, far = (y + 1) % 4, (y + 3) % 4, (y + 2) % 4
    mine, other = zl * 4, (1 - zl) * 4
    to_z, to_p, to_m = (other + y, d), (mine + up, d), (mine + down, d)

    def dev_at(z, n):
        return ((n // 2) * 4 + z) * 2 + n % 2

    barrier = pltpu.get_barrier_semaphore()

    def greet(i, _):
        who = dev_at((zh + 2 + i // NEAR) % 4, (xc + 4 + i) % NEAR)

        @pl.when(who != d)
        def _():
            pl.semaphore_signal(barrier, inc=1, device_id=(g, who), device_id_type=MESH)
        return 0

    lax.fori_loop(0, ND, greet, 0)
    for who in (to_z, to_p, to_m):
        pl.semaphore_signal(barrier, inc=1, device_id=who, device_id_type=MESH)

    row = lax.broadcasted_iota(I32, (ROWS, 128), 0)
    lane = lax.broadcasted_iota(I32, (ROWS, 128), 1)

    def quantise(i):
        qs = [q_ref[:, 2 * i + h, :] for h in range(2)]
        os = [o_ref[:, 2 * i + h, :] for h in range(2)]
        ks = [kv_ref[i, 2 * h:2 * h + 2, :] for h in range(4)]
        blocks = (
            jnp.concatenate([qs[0], qs[1], ks[0], ks[2]], axis=0),
            jnp.concatenate([os[0], ks[1]], axis=0),
            jnp.concatenate([os[1], ks[3]], axis=0),
        )
        codes, packed = [], jnp.zeros((1, 128), F32)
        for t, x in enumerate(blocks):
            top = jnp.max(jnp.abs(x), axis=1, keepdims=True)
            scale = jnp.maximum((top * GROW).astype(BF16).astype(F32), LEAST)
            codes.append(jnp.round(x * (1.0 / scale)).astype(I32).astype(jnp.int16))
            spread = jnp.where(lane == row + ROWS * ((t + g) % NG), scale, 0.0)
            packed = packed + jnp.sum(spread, axis=0, keepdims=True)
        return codes, packed

    def code_near(n, _):
        codes, packed = quantise(dev_at(zh, n))
        for t in range(3):
            near[t, g, n] = codes[t]
        nsc[g, n] = packed
        return 0

    def code_far(n, _):
        codes, packed = quantise(dev_at((zh + 1 + n // NEAR) % 4, n % NEAR))
        for t in range(3):
            send[t, n] = codes[t]
        ssend[n] = packed
        return 0

    for c in loads:
        c.wait()
    lax.fori_loop(0, FAR, code_far, 0, unroll=4)
    lax.fori_loop(0, NEAR, code_near, 0, unroll=4)
    pl.semaphore_wait(barrier, ND + 2)

    def into(part, group):
        if part < 4:
            return nsc.at[group] if part == 3 else near.at[part, group]
        ref = gsc.at[group] if part == 7 else gat.at[part - 4, group]
        return ref.at[pl.ds(NEAR, FAR)]

    def half(part, group, n):
        size = (NEAR if part < 4 else FAR) // 2
        return into(part, group).at[pl.ds(n * size, size)]

    def hop(part, kind, ref, who):
        n = part * 9 + kind
        return pltpu.make_async_remote_copy(
            src_ref=ref, dst_ref=ref, send_sem=s_send.at[n], recv_sem=s_recv.at[n],
            device_id=who, device_id_type=MESH)

    started = []

    def go(*args):
        c = hop(*args)
        c.start()
        started.append(c)

    def own(part):
        own_z(part)
        own_y(part)

    def own_z(part):
        go(part, 0, into(part, g), to_z)

    def own_y(part):
        go(part, 1, into(part, g), to_p)
        go(part, 2, into(part, g), to_m)

    def partner(part):
        ref = into(part, other + y)
        hop(part, 0, ref, to_z).wait_recv()
        go(part, 3, ref, to_p)
        go(part, 4, ref, to_m)

    def forward(part, b):
        base = (mine, other)[b]
        hop(part, 1 + 2 * b, into(part, base + down), to_p).wait_recv()
        go(part, 5 + 2 * b, half(part, base + down, 0), to_p)
        hop(part, 2 + 2 * b, into(part, base + up), to_m).wait_recv()
        go(part, 6 + 2 * b, half(part, base + up, 1), to_m)

    def finish(part):
        for b, base in enumerate((mine, other)):
            hop(part, 5 + 2 * b, half(part, base + far, 0), to_p).wait_recv()
            hop(part, 6 + 2 * b, half(part, base + far, 1), to_m).wait_recv()

    def cross(part):
        go(part, 3, into(part, mine + down), to_z)
        go(part, 4, into(part, mine + up), to_z)

    def cross_far(part):
        hop(part, 5, half(part, mine + far, 0), to_p).wait_recv()
        hop(part, 6, half(part, mine + far, 1), to_m).wait_recv()
        go(part, 7, into(part, mine + far), to_z)

    def finish_cross(part):
        for kind, group in ((0, y), (3, down), (4, up), (7, far)):
            hop(part, kind, into(part, other + group), to_z).wait_recv()

    def far_out(t):
        src = ssend if t == 3 else send.at[t]
        dst = gsc.at[g] if t == 3 else gat.at[t, g]

        def one(k, _):
            rel, n = k // NEAR, (xc + k) % NEAR
            pltpu.make_async_remote_copy(
                src_ref=src.at[rel * NEAR + n], dst_ref=dst.at[NEAR + (2 - rel) * NEAR + xc],
                send_sem=a_send.at[t], recv_sem=a_recv.at[t],
                device_id=(g, dev_at((zh + 1 + rel) % 4, n)), device_id_type=MESH).start()
            return 0

        lax.fori_loop(0, FAR, one, 0)

    def far_in(t):
        whole = into(t + 4, g)
        pltpu.make_async_copy(whole, whole, a_recv.at[t]).wait()

    def near_out(t):
        src = nsc if t == 3 else near.at[t]
        dst = gsc if t == 3 else gat.at[t]

        def one(k, _):
            n = (xc + k) % NEAR
            pltpu.make_async_remote_copy(
                src_ref=src.at[:, n], dst_ref=dst.at[:, xc],
                send_sem=x_send.at[t], recv_sem=x_recv.at[t],
                device_id=(g, dev_at(zh, n)), device_id_type=MESH).start()
            return 0

        lax.fori_loop(1, NEAR, one, 0)
        for n in range(NG):
            if t == 3:
                gsc[n, xc] = nsc[n, xc]
            else:
                gat[t, n, xc] = near[t, n, xc]

    def near_in(t):
        whole = (gsc if t == 3 else gat.at[t]).at[:, pl.ds(0, NEAR - 1)]
        pltpu.make_async_copy(whole, whole, x_recv.at[t]).wait()

    def maps():
        r = lax.broadcasted_iota(I32, (128, 128), 0)
        k = lax.broadcasted_iota(I32, (128, 128), 1)
        kin = k - (k // ROWS) * ROWS

        def piece(rem, size):
            return sum(((rem >= size * n).astype(I32) for n in range(1, NG)), jnp.zeros_like(rem))

        h1 = (r >= 48).astype(I32)
        rq = r - 48 * h1
        jq = piece(rq, 6)
        h2 = (r >= 112).astype(I32)
        rk = r - 96 - 16 * h2
        jk = piece(rk, 2)
        offset = jnp.where(r < 96, rq - 6 * jq + 6 * h1, rk - 2 * jk + 12 + 2 * h2)
        jmap[0] = jnp.where(offset == kin, jnp.where(r < 96, jq, jk), -1)
        jo = piece(r, 14)
        rv = r - 112
        jv = piece(rv, 2)
        offset = jnp.where(r < 112, r - 14 * jo, rv - 2 * jv + 14)
        jmap[1] = jnp.where(offset == kin, jnp.where(r < 112, jo, jv), -1)
        kg = lax.broadcasted_iota(I32, (ND, 128), 1) // ROWS
        held = jnp.zeros((ND, 128), I32)
        owner = own_ref[...].T
        for j in range(NG):
            held = held + jnp.where(owner[:, j:j + 1] == kg, j, 0)
        inv[...] = held

    def scales():
        at = lax.broadcasted_iota(I32, (ND, 128), 1) // ROWS
        lines = [gsc[n].reshape(ND, 128) for n in range(NG)]
        for t in range(3):
            held = jnp.zeros((ND, 128), F32)
            for n in range(NG):
                held = held + jnp.where(at == (n + t) % NG, lines[n], 0.0)
            sca[t] = pltpu.roll(held, (128 - ROWS * t) % 128, 1)

    def decode(t, pos):
        i = dev_at((zh + pos // NEAR) % 4, pos % NEAR)
        code = gat[t, :, pos].reshape(128, 128).astype(F32)
        hi = code.astype(BF16)
        lo = (code - hi.astype(F32)).astype(BF16)
        pick = jnp.where(jmap[min(t, 1)] == inv[pl.ds(i, 1), :], sca[t, pl.ds(pos, 1), :], 0.0).astype(BF16)
        x = jnp.dot(jnp.concatenate([pick, pick], axis=1), jnp.concatenate([hi, lo], axis=0),
                    preferred_element_type=F32)
        hi = x.astype(BF16)
        return i, hi, (x - hi.astype(F32)).astype(BF16)

    def over(first, last, one):
        lax.fori_loop(first, last, one, 0, unroll=min(12, last - first))

    def decode_q(first, last):
        def one(pos, _):
            i, hi, lo = decode(0, pos)
            at = pl.ds(pl.multiple_of(i * 48, 16), 48)
            kat = pl.ds(pl.multiple_of(i * 16, 16), 16)
            for h in range(2):
                qm[h, at, 0:128] = hi[48 * h:48 * h + 48]
                qm[h, at, 128:256] = lo[48 * h:48 * h + 48]
                km[h, kat, 0:128] = hi[96 + 16 * h:112 + 16 * h]
                km[h, kat, 128:256] = lo[96 + 16 * h:112 + 16 * h]
            return 0

        over(first, last, one)

    def fold_q(h):
        qf_ref[h] = fold(qm[h], km[h])

    def decode_o(h, first, last):
        om, vm = ((om0, vm0), (om1, vm1))[h]

        def one(pos, _):
            i, hi, lo = decode(1 + h, pos)
            at = pl.ds(pl.multiple_of(i * 112, 16), 112)
            vat = pl.ds(pl.multiple_of(i * 16, 16), 16)
            om[at, 0:128] = hi[:112]
            om[at, 128:256] = lo[:112]
            vm[vat, 0:128] = hi[112:]
            vm[vat, 128:256] = lo[112:]
            return 0

        over(first, last, one)

    def fold_o():
        def tile(i, _):
            at = pl.ds(pl.multiple_of(i * 256, 256), 256)
            of_ref[:, at] = fold(vm0[...], om0[at])
            return 0

        lax.fori_loop(0, 14, tile, 0, unroll=14)

    order = (3, 0, 1, 2)
    for t in order:
        own(t)
    far_out(0)
    far_out(3)
    for t in order:
        forward(t, 0)
    for t in order:
        partner(t)
    far_out(1)
    far_out(2)
    maps()
    for t in order:
        forward(t, 1)
    far_in(0)
    own(4)
    far_in(3)
    own(7)
    for t in order:
        finish(t)
        near_out(t)
    far_in(1)
    own(5)
    forward(7, 0)
    forward(4, 0)
    partner(7)
    partner(4)
    far_in(2)
    own(6)
    forward(7, 1)
    forward(4, 1)
    forward(5, 0)
    partner(5)
    forward(6, 0)
    partner(6)
    finish(7)
    near_in(3)
    scales()
    near_in(0)
    decode_q(0, NEAR)
    near_in(1)
    decode_o(0, 0, NEAR)
    near_in(2)
    decode_o(1, 0, NEAR)
    finish(4)
    decode_q(NEAR, ND)
    forward(5, 1)
    fold_q(0)
    forward(6, 1)
    fold_q(1)
    finish(5)
    decode_o(0, NEAR, ND)
    fold_o()
    finish(6)
    decode_o(1, NEAR, ND)
    for c in started:
        c.wait_send()
    for t in range(4):
        sent = ssend if t == 3 else send.at[t]
        pltpu.make_async_copy(sent, sent, a_send.at[t]).wait()
        sent = (nsc if t == 3 else near.at[t]).at[:, pl.ds(0, NEAR - 1)]
        pltpu.make_async_copy(sent, sent, x_send.at[t]).wait()


def last_kernel(qf_ref, of_ref, om, vm, q_out, o_out, held, sem):
    whole = (pltpu.make_async_copy(qf_ref, q_out, sem.at[0]), pltpu.make_async_copy(of_ref, o_out.at[0], sem.at[1]))
    for c in whole:
        c.start()

    def out(i):
        at = pl.ds(pl.multiple_of(i * 256, 256), 256)
        return at, pltpu.make_async_copy(held.at[:, at], o_out.at[1, :, at], sem.at[2 + i])

    def tile(i, _):
        at, c = out(i)
        held[:, at] = fold(vm[...], om[at])
        c.start()
        return 0

    lax.fori_loop(0, 14, tile, 0, unroll=14)

    def done(i, _):
        out(i)[1].wait()
        return 0

    lax.fori_loop(0, 14, done, 0)
    for c in whole:
        c.wait()


def body(stored_q, stored_kv, stored_o, owner_map):
    vmem = pl.BlockSpec(memory_space=pltpu.VMEM)
    hbm = pl.BlockSpec(memory_space=pltpu.HBM)
    dma = pltpu.SemaphoreType.DMA
    far_inputs = [pltpu.with_memory_space_constraint(x, pltpu.HBM) for x in (
        stored_q.reshape(6, 64, 128),
        stored_kv.reshape(2, ND, 4, 128).transpose(1, 2, 0, 3).reshape(ND, 8, 128),
        stored_o.reshape(14, 64, 128),
        owner_map.T)]
    parts = pl.pallas_call(
        kernel,
        out_shape=(pltpu.VMEM((2, 1536, 512), BF16), pltpu.VMEM((512, 3584), BF16),
                   pltpu.VMEM((3584, 256), BF16), pltpu.VMEM((512, 256), BF16)),
        in_specs=[hbm] * 4,
        out_specs=[vmem] * 4,
        scratch_shapes=[
            pltpu.VMEM((6, 64, 128), F32),
            pltpu.VMEM((ND, 8, 128), F32),
            pltpu.VMEM((14, 64, 128), F32),
            pltpu.VMEM((NG, ND), I32),
            pltpu.VMEM((3, NG, NEAR, ROWS, 128), jnp.int16),
            pltpu.VMEM((NG, NEAR, 1, 128), F32),
            pltpu.VMEM((3, FAR, ROWS, 128), jnp.int16),
            pltpu.VMEM((FAR, 1, 128), F32),
            pltpu.VMEM((3, NG, ND, ROWS, 128), jnp.int16),
            pltpu.VMEM((NG, ND, 1, 128), F32),
            pltpu.VMEM((3, ND, 128), F32),
            pltpu.VMEM((2, 128, 128), I32),
            pltpu.VMEM((ND, 128), I32),
            pltpu.VMEM((2, 1536, 256), BF16),
            pltpu.VMEM((2, 512, 256), BF16),
            pltpu.VMEM((3584, 256), BF16),
            pltpu.VMEM((512, 256), BF16),
            dma((4,)), dma((4,)), dma((4,)), dma((4,)), dma((4,)), dma((72,)), dma((72,)),
        ],
        compiler_params=pltpu.CompilerParams(
            collective_id=0, has_side_effects=True, vmem_limit_bytes=32 * 1024 * 1024),
    )(*far_inputs)
    return pl.pallas_call(
        last_kernel,
        out_shape=(jax.ShapeDtypeStruct((2, 1536, 512), BF16), jax.ShapeDtypeStruct((2, 512, 3584), BF16)),
        in_specs=[vmem] * 4,
        out_specs=[hbm] * 2,
        scratch_shapes=[pltpu.VMEM((512, 3584), BF16), dma((16,))],
        compiler_params=pltpu.CompilerParams(vmem_limit_bytes=32 * 1024 * 1024),
    )(*parts)


def solution(mesh):
    in_specs = (P("group", "dev", None), P("group", "dev", None), P("group", "dev", None), P())
    out_specs = (P("dev", None, None), P("dev", None, None))
    return jax.shard_map(body, mesh=mesh, in_specs=in_specs, out_specs=out_specs, check_vma=False)
```

```python
import jax
import jax.numpy as jnp
from jax import lax
from jax.experimental import pallas as pl
from jax.experimental.pallas import tpu as pltpu
from jax.sharding import PartitionSpec as P

MESH = pl.DeviceIdType.MESH
F32, BF16, I32 = jnp.float32, jnp.bfloat16, jnp.int32
NG, ND = 8, 32
ROWS = 16
NEAR, FAR = 8, 24
GROW = 1.008 / 32767.0
LEAST = 2.0**-120


def nt(a, b):
    return lax.dot_general(a, b, (((1,), (1,)), ((), ())), preferred_element_type=F32)


def fold(a, b):
    hi = b[:, 0:128]
    return (nt(a, jnp.concatenate([hi, hi], axis=1)) + nt(a[:, 0:128], b[:, 128:256])).astype(BF16)


def kernel(q_hbm, kv_hbm, o_hbm, own_hbm, qf_ref, of_ref, om1, vm1,
           q_ref, kv_ref, o_ref, own_ref, near, nsc, send, ssend, gat, gsc, sca, jmap, inv, qm, km, om0, vm0,
           in_sem, a_send, a_recv, x_send, x_recv, s_send, s_recv):
    loads = [pltpu.make_async_copy(a, b, in_sem.at[n])
             for n, (a, b) in enumerate(((q_hbm, q_ref), (kv_hbm, kv_ref), (o_hbm, o_ref), (own_hbm, own_ref)))]
    for c in loads:
        c.start()
    g = lax.axis_index("group")
    d = lax.axis_index("dev")
    zl, y = g // 4, g % 4
    zh, xc = (d // 2) % 4, (d // 8) * 2 + d % 2
    up, down, far = (y + 1) % 4, (y + 3) % 4, (y + 2) % 4
    mine, other = zl * 4, (1 - zl) * 4
    to_z, to_p, to_m = (other + y, d), (mine + up, d), (mine + down, d)

    def dev_at(z, n):
        return ((n // 2) * 4 + z) * 2 + n % 2

    barrier = pltpu.get_barrier_semaphore()

    def greet(i, _):
        who = dev_at((zh + 2 + i // NEAR) % 4, (xc + 4 + i) % NEAR)

        @pl.when(who != d)
        def _():
            pl.semaphore_signal(barrier, inc=1, device_id=(g, who), device_id_type=MESH)
        return 0

    lax.fori_loop(0, ND, greet, 0)
    for who in (to_z, to_p, to_m):
        pl.semaphore_signal(barrier, inc=1, device_id=who, device_id_type=MESH)

    row = lax.broadcasted_iota(I32, (ROWS, 128), 0)
    lane = lax.broadcasted_iota(I32, (ROWS, 128), 1)

    def quantise(i):
        qs = [q_ref[:, 2 * i + h, :] for h in range(2)]
        os = [o_ref[:, 2 * i + h, :] for h in range(2)]
        ks = [kv_ref[i, 2 * h:2 * h + 2, :] for h in range(4)]
        blocks = (
            jnp.concatenate([qs[0], qs[1], ks[0], ks[2]], axis=0),
            jnp.concatenate([os[0], ks[1]], axis=0),
            jnp.concatenate([os[1], ks[3]], axis=0),
        )
        codes, packed = [], jnp.zeros((1, 128), F32)
        for t, x in enumerate(blocks):
            top = jnp.max(jnp.abs(x), axis=1, keepdims=True)
            scale = jnp.maximum((top * GROW).astype(BF16).astype(F32), LEAST)
            codes.append(jnp.round(x * (1.0 / scale)).astype(I32).astype(jnp.int16))
            spread = jnp.where(lane == row + ROWS * ((t + g) % NG), scale, 0.0)
            packed = packed + jnp.sum(spread, axis=0, keepdims=True)
        return codes, packed

    def code_near(n, _):
        codes, packed = quantise(dev_at(zh, n))
        for t in range(3):
            near[t, g, n] = codes[t]
        nsc[g, n] = packed
        return 0

    def code_far(n, _):
        codes, packed = quantise(dev_at((zh + 1 + n // NEAR) % 4, n % NEAR))
        for t in range(3):
            send[t, n] = codes[t]
        ssend[n] = packed
        return 0

    for c in loads:
        c.wait()
    lax.fori_loop(0, FAR, code_far, 0, unroll=4)
    lax.fori_loop(0, NEAR, code_near, 0, unroll=4)
    pl.semaphore_wait(barrier, ND + 2)

    def into(part, group):
        if part < 4:
            return nsc.at[group] if part == 3 else near.at[part, group]
        ref = gsc.at[group] if part == 7 else gat.at[part - 4, group]
        return ref.at[pl.ds(NEAR, FAR)]

    def half(part, group, n):
        size = (NEAR if part < 4 else FAR) // 2
        return into(part, group).at[pl.ds(n * size, size)]

    def hop(part, kind, ref, who):
        n = part * 9 + kind
        return pltpu.make_async_remote_copy(
            src_ref=ref, dst_ref=ref, send_sem=s_send.at[n], recv_sem=s_recv.at[n],
            device_id=who, device_id_type=MESH)

    started = []

    def go(*args):
        c = hop(*args)
        c.start()
        started.append(c)

    def own(part):
        own_z(part)
        own_y(part)

    def own_z(part):
        go(part, 0, into(part, g), to_z)

    def own_y(part):
        go(part, 1, into(part, g), to_p)
        go(part, 2, into(part, g), to_m)

    def partner(part):
        ref = into(part, other + y)
        hop(part, 0, ref, to_z).wait_recv()
        go(part, 3, ref, to_p)
        go(part, 4, ref, to_m)

    def forward(part, b):
        base = (mine, other)[b]
        hop(part, 1 + 2 * b, into(part, base + down), to_p).wait_recv()
        go(part, 5 + 2 * b, half(part, base + down, 0), to_p)
        hop(part, 2 + 2 * b, into(part, base + up), to_m).wait_recv()
        go(part, 6 + 2 * b, half(part, base + up, 1), to_m)

    def finish(part):
        for b, base in enumerate((mine, other)):
            hop(part, 5 + 2 * b, half(part, base + far, 0), to_p).wait_recv()
            hop(part, 6 + 2 * b, half(part, base + far, 1), to_m).wait_recv()

    def cross(part):
        go(part, 3, into(part, mine + down), to_z)
        go(part, 4, into(part, mine + up), to_z)

    def cross_far(part):
        hop(part, 5, half(part, mine + far, 0), to_p).wait_recv()
        hop(part, 6, half(part, mine + far, 1), to_m).wait_recv()
        go(part, 7, into(part, mine + far), to_z)

    def finish_cross(part):
        for kind, group in ((0, y), (3, down), (4, up), (7, far)):
            hop(part, kind, into(part, other + group), to_z).wait_recv()

    def far_out(t):
        src = ssend if t == 3 else send.at[t]
        dst = gsc.at[g] if t == 3 else gat.at[t, g]

        def one(k, _):
            rel, n = k // NEAR, (xc + k) % NEAR
            pltpu.make_async_remote_copy(
                src_ref=src.at[rel * NEAR + n], dst_ref=dst.at[NEAR + (2 - rel) * NEAR + xc],
                send_sem=a_send.at[t], recv_sem=a_recv.at[t],
                device_id=(g, dev_at((zh + 1 + rel) % 4, n)), device_id_type=MESH).start()
            return 0

        lax.fori_loop(0, FAR, one, 0)

    def far_in(t):
        whole = into(t + 4, g)
        pltpu.make_async_copy(whole, whole, a_recv.at[t]).wait()

    def near_out(t):
        src = nsc if t == 3 else near.at[t]
        dst = gsc if t == 3 else gat.at[t]

        def one(k, _):
            n = (xc + k) % NEAR
            pltpu.make_async_remote_copy(
                src_ref=src.at[:, n], dst_ref=dst.at[:, xc],
                send_sem=x_send.at[t], recv_sem=x_recv.at[t],
                device_id=(g, dev_at(zh, n)), device_id_type=MESH).start()
            return 0

        lax.fori_loop(1, NEAR, one, 0)
        for n in range(NG):
            if t == 3:
                gsc[n, xc] = nsc[n, xc]
            else:
                gat[t, n, xc] = near[t, n, xc]

    def near_in(t):
        whole = (gsc if t == 3 else gat.at[t]).at[:, pl.ds(0, NEAR - 1)]
        pltpu.make_async_copy(whole, whole, x_recv.at[t]).wait()

    def maps():
        r = lax.broadcasted_iota(I32, (128, 128), 0)
        k = lax.broadcasted_iota(I32, (128, 128), 1)
        kin = k - (k // ROWS) * ROWS

        def piece(rem, size):
            return sum(((rem >= size * n).astype(I32) for n in range(1, NG)), jnp.zeros_like(rem))

        h1 = (r >= 48).astype(I32)
        rq = r - 48 * h1
        jq = piece(rq, 6)
        h2 = (r >= 112).astype(I32)
        rk = r - 96 - 16 * h2
        jk = piece(rk, 2)
        offset = jnp.where(r < 96, rq - 6 * jq + 6 * h1, rk - 2 * jk + 12 + 2 * h2)
        jmap[0] = jnp.where(offset == kin, jnp.where(r < 96, jq, jk), -1)
        jo = piece(r, 14)
        rv = r - 112
        jv = piece(rv, 2)
        offset = jnp.where(r < 112, r - 14 * jo, rv - 2 * jv + 14)
        jmap[1] = jnp.where(offset == kin, jnp.where(r < 112, jo, jv), -1)
        kg = lax.broadcasted_iota(I32, (ND, 128), 1) // ROWS
        held = jnp.zeros((ND, 128), I32)
        owner = own_ref[...].T
        for j in range(NG):
            held = held + jnp.where(owner[:, j:j + 1] == kg, j, 0)
        inv[...] = held

    def scales():
        at = lax.broadcasted_iota(I32, (ND, 128), 1) // ROWS
        lines = [gsc[n].reshape(ND, 128) for n in range(NG)]
        for t in range(3):
            held = jnp.zeros((ND, 128), F32)
            for n in range(NG):
                held = held + jnp.where(at == (n + t) % NG, lines[n], 0.0)
            sca[t] = pltpu.roll(held, (128 - ROWS * t) % 128, 1)

    def decode(t, pos):
        i = dev_at((zh + pos // NEAR) % 4, pos % NEAR)
        code = gat[t, :, pos].reshape(128, 128).astype(F32)
        hi = code.astype(BF16)
        lo = (code - hi.astype(F32)).astype(BF16)
        pick = jnp.where(jmap[min(t, 1)] == inv[pl.ds(i, 1), :], sca[t, pl.ds(pos, 1), :], 0.0).astype(BF16)
        x = jnp.dot(jnp.concatenate([pick, pick], axis=1), jnp.concatenate([hi, lo], axis=0),
                    preferred_element_type=F32)
        hi = x.astype(BF16)
        return i, hi, (x - hi.astype(F32)).astype(BF16)

    def over(first, last, one):
        lax.fori_loop(first, last, one, 0, unroll=min(12, last - first))

    def decode_q(first, last):
        def one(pos, _):
            i, hi, lo = decode(0, pos)
            at = pl.ds(pl.multiple_of(i * 48, 16), 48)
            kat = pl.ds(pl.multiple_of(i * 16, 16), 16)
            for h in range(2):
                qm[h, at, 0:128] = hi[48 * h:48 * h + 48]
                qm[h, at, 128:256] = lo[48 * h:48 * h + 48]
                km[h, kat, 0:128] = hi[96 + 16 * h:112 + 16 * h]
                km[h, kat, 128:256] = lo[96 + 16 * h:112 + 16 * h]
            return 0

        over(first, last, one)

    def fold_q(h):
        qf_ref[h] = fold(qm[h], km[h])

    def decode_o(h, first, last):
        om, vm = ((om0, vm0), (om1, vm1))[h]

        def one(pos, _):
            i, hi, lo = decode(1 + h, pos)
            at = pl.ds(pl.multiple_of(i * 112, 16), 112)
            vat = pl.ds(pl.multiple_of(i * 16, 16), 16)
            om[at, 0:128] = hi[:112]
            om[at, 128:256] = lo[:112]
            vm[vat, 0:128] = hi[112:]
            vm[vat, 128:256] = lo[112:]
            return 0

        over(first, last, one)

    def fold_o():
        def tile(i, _):
            at = pl.ds(pl.multiple_of(i * 256, 256), 256)
            of_ref[:, at] = fold(vm0[...], om0[at])
            return 0

        lax.fori_loop(0, 14, tile, 0, unroll=14)

    order = (3, 0, 1, 2)
    for t in order:
        own(t)
    far_out(0)
    far_out(3)
    for t in order:
        forward(t, 0)
    for t in order:
        partner(t)
    far_out(1)
    far_out(2)
    maps()
    for t in order:
        forward(t, 1)
    far_in(0)
    own(4)
    far_in(3)
    own(7)
    for t in order:
        finish(t)
        near_out(t)
    far_in(1)
    own(5)
    forward(7, 0)
    forward(4, 0)
    partner(7)
    partner(4)
    far_in(2)
    own(6)
    forward(5, 0)
    cross(5)
    forward(7, 1)
    forward(4, 1)
    forward(6, 0)
    partner(6)
    cross_far(5)
    finish(7)
    near_in(3)
    scales()
    near_in(0)
    decode_q(0, NEAR)
    near_in(1)
    decode_o(0, 0, NEAR)
    near_in(2)
    decode_o(1, 0, NEAR)
    finish(4)
    decode_q(NEAR, ND)
    fold_q(0)
    forward(6, 1)
    fold_q(1)
    finish_cross(5)
    decode_o(0, NEAR, ND)
    fold_o()
    finish(6)
    decode_o(1, NEAR, ND)
    for c in started:
        c.wait_send()
    for t in range(4):
        sent = ssend if t == 3 else send.at[t]
        pltpu.make_async_copy(sent, sent, a_send.at[t]).wait()
        sent = (nsc if t == 3 else near.at[t]).at[:, pl.ds(0, NEAR - 1)]
        pltpu.make_async_copy(sent, sent, x_send.at[t]).wait()


def last_kernel(qf_ref, of_ref, om, vm, q_out, o_out, held, sem):
    whole = (pltpu.make_async_copy(qf_ref, q_out, sem.at[0]), pltpu.make_async_copy(of_ref, o_out.at[0], sem.at[1]))
    for c in whole:
        c.start()

    def out(i):
        at = pl.ds(pl.multiple_of(i * 256, 256), 256)
        return at, pltpu.make_async_copy(held.at[:, at], o_out.at[1, :, at], sem.at[2 + i])

    def tile(i, _):
        at, c = out(i)
        held[:, at] = fold(vm[...], om[at])
        c.start()
        return 0

    lax.fori_loop(0, 14, tile, 0, unroll=14)

    def done(i, _):
        out(i)[1].wait()
        return 0

    lax.fori_loop(0, 14, done, 0)
    for c in whole:
        c.wait()


def body(stored_q, stored_kv, stored_o, owner_map):
    vmem = pl.BlockSpec(memory_space=pltpu.VMEM)
    hbm = pl.BlockSpec(memory_space=pltpu.HBM)
    dma = pltpu.SemaphoreType.DMA
    far_inputs = [pltpu.with_memory_space_constraint(x, pltpu.HBM) for x in (
        stored_q.reshape(6, 64, 128),
        stored_kv.reshape(2, ND, 4, 128).transpose(1, 2, 0, 3).reshape(ND, 8, 128),
        stored_o.reshape(14, 64, 128),
        owner_map.T)]
    parts = pl.pallas_call(
        kernel,
        out_shape=(pltpu.VMEM((2, 1536, 512), BF16), pltpu.VMEM((512, 3584), BF16),
                   pltpu.VMEM((3584, 256), BF16), pltpu.VMEM((512, 256), BF16)),
        in_specs=[hbm] * 4,
        out_specs=[vmem] * 4,
        scratch_shapes=[
            pltpu.VMEM((6, 64, 128), F32),
            pltpu.VMEM((ND, 8, 128), F32),
            pltpu.VMEM((14, 64, 128), F32),
            pltpu.VMEM((NG, ND), I32),
            pltpu.VMEM((3, NG, NEAR, ROWS, 128), jnp.int16),
            pltpu.VMEM((NG, NEAR, 1, 128), F32),
            pltpu.VMEM((3, FAR, ROWS, 128), jnp.int16),
            pltpu.VMEM((FAR, 1, 128), F32),
            pltpu.VMEM((3, NG, ND, ROWS, 128), jnp.int16),
            pltpu.VMEM((NG, ND, 1, 128), F32),
            pltpu.VMEM((3, ND, 128), F32),
            pltpu.VMEM((2, 128, 128), I32),
            pltpu.VMEM((ND, 128), I32),
            pltpu.VMEM((2, 1536, 256), BF16),
            pltpu.VMEM((2, 512, 256), BF16),
            pltpu.VMEM((3584, 256), BF16),
            pltpu.VMEM((512, 256), BF16),
            dma((4,)), dma((4,)), dma((4,)), dma((4,)), dma((4,)), dma((72,)), dma((72,)),
        ],
        compiler_params=pltpu.CompilerParams(
            collective_id=0, has_side_effects=True, vmem_limit_bytes=32 * 1024 * 1024),
    )(*far_inputs)
    return pl.pallas_call(
        last_kernel,
        out_shape=(jax.ShapeDtypeStruct((2, 1536, 512), BF16), jax.ShapeDtypeStruct((2, 512, 3584), BF16)),
        in_specs=[vmem] * 4,
        out_specs=[hbm] * 2,
        scratch_shapes=[pltpu.VMEM((512, 3584), BF16), dma((16,))],
        compiler_params=pltpu.CompilerParams(vmem_limit_bytes=32 * 1024 * 1024),
    )(*parts)


def solution(mesh):
    in_specs = (P("group", "dev", None), P("group", "dev", None), P("group", "dev", None), P())
    out_specs = (P("dev", None, None), P("dev", None, None))
    return jax.shard_map(body, mesh=mesh, in_specs=in_specs, out_specs=out_specs, check_vma=False)
```

```python
import jax
import jax.numpy as jnp
from jax import lax
from jax.experimental import pallas as pl
from jax.experimental.pallas import tpu as pltpu
from jax.sharding import PartitionSpec as P

MESH = pl.DeviceIdType.MESH
F32, BF16, I32 = jnp.float32, jnp.bfloat16, jnp.int32
NG, ND = 8, 32
ROWS = 16
TILES, EARLY = 14, 7
NEAR, FAR = 8, 24
GROW = 1.008 / 32767.0
LEAST = 2.0**-120


def nt(a, b):
    return lax.dot_general(a, b, (((1,), (1,)), ((), ())), preferred_element_type=F32)


def fold(a, b):
    hi = b[:, 0:128]
    return (nt(a, jnp.concatenate([hi, hi], axis=1)) + nt(a[:, 0:128], b[:, 128:256])).astype(BF16)


def kernel(q_hbm, kv_hbm, o_hbm, own_hbm, qf_ref, of_ref, om0, vm0, om1, vm1,
           q_ref, kv_ref, o_ref, own_ref, near, nsc, send, ssend, gat, gsc, sca, jmap, inv, qm, km,
           in_sem, a_send, a_recv, x_send, x_recv, s_send, s_recv):
    loads = [pltpu.make_async_copy(a, b, in_sem.at[n])
             for n, (a, b) in enumerate(((q_hbm, q_ref), (kv_hbm, kv_ref), (o_hbm, o_ref), (own_hbm, own_ref)))]
    for c in loads:
        c.start()
    g = lax.axis_index("group")
    d = lax.axis_index("dev")
    zl, y = g // 4, g % 4
    zh, xc = (d // 2) % 4, (d // 8) * 2 + d % 2
    up, down, far = (y + 1) % 4, (y + 3) % 4, (y + 2) % 4
    mine, other = zl * 4, (1 - zl) * 4
    to_z, to_p, to_m = (other + y, d), (mine + up, d), (mine + down, d)

    def dev_at(z, n):
        return ((n // 2) * 4 + z) * 2 + n % 2

    barrier = pltpu.get_barrier_semaphore()

    def greet(i, _):
        who = dev_at((zh + 2 + i // NEAR) % 4, (xc + 4 + i) % NEAR)

        @pl.when(who != d)
        def _():
            pl.semaphore_signal(barrier, inc=1, device_id=(g, who), device_id_type=MESH)
        return 0

    lax.fori_loop(0, ND, greet, 0)
    for who in (to_z, to_p, to_m):
        pl.semaphore_signal(barrier, inc=1, device_id=who, device_id_type=MESH)

    row = lax.broadcasted_iota(I32, (ROWS, 128), 0)
    lane = lax.broadcasted_iota(I32, (ROWS, 128), 1)

    def quantise(i):
        qs = [q_ref[:, 2 * i + h, :] for h in range(2)]
        os = [o_ref[:, 2 * i + h, :] for h in range(2)]
        ks = [kv_ref[i, 2 * h:2 * h + 2, :] for h in range(4)]
        blocks = (
            jnp.concatenate([qs[0], qs[1], ks[0], ks[2]], axis=0),
            jnp.concatenate([os[0], ks[1]], axis=0),
            jnp.concatenate([os[1], ks[3]], axis=0),
        )
        codes, packed = [], jnp.zeros((1, 128), F32)
        for t, x in enumerate(blocks):
            top = jnp.max(jnp.abs(x), axis=1, keepdims=True)
            scale = jnp.maximum((top * GROW).astype(BF16).astype(F32), LEAST)
            codes.append(jnp.round(x * (1.0 / scale)).astype(I32).astype(jnp.int16))
            spread = jnp.where(lane == row + ROWS * ((t + g) % NG), scale, 0.0)
            packed = packed + jnp.sum(spread, axis=0, keepdims=True)
        return codes, packed

    def code_near(n, _):
        codes, packed = quantise(dev_at(zh, n))
        for t in range(3):
            near[t, g, n] = codes[t]
        nsc[g, n] = packed
        return 0

    def code_far(n, _):
        codes, packed = quantise(dev_at((zh + 1 + n // NEAR) % 4, n % NEAR))
        for t in range(3):
            send[t, n] = codes[t]
        ssend[n] = packed
        return 0

    for c in loads:
        c.wait()
    lax.fori_loop(0, FAR, code_far, 0, unroll=4)
    lax.fori_loop(0, NEAR, code_near, 0, unroll=4)
    pl.semaphore_wait(barrier, ND + 2)

    def into(part, group):
        if part < 4:
            return nsc.at[group] if part == 3 else near.at[part, group]
        ref = gsc.at[group] if part == 7 else gat.at[part - 4, group]
        return ref.at[pl.ds(NEAR, FAR)]

    def half(part, group, n):
        size = (NEAR if part < 4 else FAR) // 2
        return into(part, group).at[pl.ds(n * size, size)]

    def hop(part, kind, ref, who):
        n = part * 9 + kind
        return pltpu.make_async_remote_copy(
            src_ref=ref, dst_ref=ref, send_sem=s_send.at[n], recv_sem=s_recv.at[n],
            device_id=who, device_id_type=MESH)

    started = []

    def go(*args):
        c = hop(*args)
        c.start()
        started.append(c)

    def own(part):
        own_z(part)
        own_y(part)

    def own_z(part):
        go(part, 0, into(part, g), to_z)

    def own_y(part):
        go(part, 1, into(part, g), to_p)
        go(part, 2, into(part, g), to_m)

    def partner(part):
        ref = into(part, other + y)
        hop(part, 0, ref, to_z).wait_recv()
        go(part, 3, ref, to_p)
        go(part, 4, ref, to_m)

    def forward(part, b):
        base = (mine, other)[b]
        hop(part, 1 + 2 * b, into(part, base + down), to_p).wait_recv()
        go(part, 5 + 2 * b, half(part, base + down, 0), to_p)
        hop(part, 2 + 2 * b, into(part, base + up), to_m).wait_recv()
        go(part, 6 + 2 * b, half(part, base + up, 1), to_m)

    def finish(part):
        for b, base in enumerate((mine, other)):
            hop(part, 5 + 2 * b, half(part, base + far, 0), to_p).wait_recv()
            hop(part, 6 + 2 * b, half(part, base + far, 1), to_m).wait_recv()

    def cross(part):
        go(part, 3, into(part, mine + down), to_z)
        go(part, 4, into(part, mine + up), to_z)

    def cross_far(part):
        hop(part, 5, half(part, mine + far, 0), to_p).wait_recv()
        hop(part, 6, half(part, mine + far, 1), to_m).wait_recv()
        go(part, 7, into(part, mine + far), to_z)

    def finish_cross(part):
        for kind, group in ((0, y), (3, down), (4, up), (7, far)):
            hop(part, kind, into(part, other + group), to_z).wait_recv()

    def far_out(t):
        src = ssend if t == 3 else send.at[t]
        dst = gsc.at[g] if t == 3 else gat.at[t, g]

        def one(k, _):
            rel, n = k // NEAR, (xc + k) % NEAR
            pltpu.make_async_remote_copy(
                src_ref=src.at[rel * NEAR + n], dst_ref=dst.at[NEAR + (2 - rel) * NEAR + xc],
                send_sem=a_send.at[t], recv_sem=a_recv.at[t],
                device_id=(g, dev_at((zh + 1 + rel) % 4, n)), device_id_type=MESH).start()
            return 0

        lax.fori_loop(0, FAR, one, 0)

    def far_in(t):
        whole = into(t + 4, g)
        pltpu.make_async_copy(whole, whole, a_recv.at[t]).wait()

    def near_out(t):
        src = nsc if t == 3 else near.at[t]
        dst = gsc if t == 3 else gat.at[t]

        def one(k, _):
            n = (xc + k) % NEAR
            pltpu.make_async_remote_copy(
                src_ref=src.at[:, n], dst_ref=dst.at[:, xc],
                send_sem=x_send.at[t], recv_sem=x_recv.at[t],
                device_id=(g, dev_at(zh, n)), device_id_type=MESH).start()
            return 0

        lax.fori_loop(1, NEAR, one, 0)
        for n in range(NG):
            if t == 3:
                gsc[n, xc] = nsc[n, xc]
            else:
                gat[t, n, xc] = near[t, n, xc]

    def near_in(t):
        whole = (gsc if t == 3 else gat.at[t]).at[:, pl.ds(0, NEAR - 1)]
        pltpu.make_async_copy(whole, whole, x_recv.at[t]).wait()

    def maps():
        r = lax.broadcasted_iota(I32, (128, 128), 0)
        k = lax.broadcasted_iota(I32, (128, 128), 1)
        kin = k - (k // ROWS) * ROWS

        def piece(rem, size):
            return sum(((rem >= size * n).astype(I32) for n in range(1, NG)), jnp.zeros_like(rem))

        h1 = (r >= 48).astype(I32)
        rq = r - 48 * h1
        jq = piece(rq, 6)
        h2 = (r >= 112).astype(I32)
        rk = r - 96 - 16 * h2
        jk = piece(rk, 2)
        offset = jnp.where(r < 96, rq - 6 * jq + 6 * h1, rk - 2 * jk + 12 + 2 * h2)
        jmap[0] = jnp.where(offset == kin, jnp.where(r < 96, jq, jk), -1)
        jo = piece(r, 14)
        rv = r - 112
        jv = piece(rv, 2)
        offset = jnp.where(r < 112, r - 14 * jo, rv - 2 * jv + 14)
        jmap[1] = jnp.where(offset == kin, jnp.where(r < 112, jo, jv), -1)
        kg = lax.broadcasted_iota(I32, (ND, 128), 1) // ROWS
        held = jnp.zeros((ND, 128), I32)
        owner = own_ref[...].T
        for j in range(NG):
            held = held + jnp.where(owner[:, j:j + 1] == kg, j, 0)
        inv[...] = held

    def scales():
        at = lax.broadcasted_iota(I32, (ND, 128), 1) // ROWS
        lines = [gsc[n].reshape(ND, 128) for n in range(NG)]
        for t in range(3):
            held = jnp.zeros((ND, 128), F32)
            for n in range(NG):
                held = held + jnp.where(at == (n + t) % NG, lines[n], 0.0)
            sca[t] = pltpu.roll(held, (128 - ROWS * t) % 128, 1)

    def decode(t, pos):
        i = dev_at((zh + pos // NEAR) % 4, pos % NEAR)
        code = gat[t, :, pos].reshape(128, 128).astype(F32)
        hi = code.astype(BF16)
        lo = (code - hi.astype(F32)).astype(BF16)
        pick = jnp.where(jmap[min(t, 1)] == inv[pl.ds(i, 1), :], sca[t, pl.ds(pos, 1), :], 0.0).astype(BF16)
        x = jnp.dot(jnp.concatenate([pick, pick], axis=1), jnp.concatenate([hi, lo], axis=0),
                    preferred_element_type=F32)
        hi = x.astype(BF16)
        return i, hi, (x - hi.astype(F32)).astype(BF16)

    def over(first, last, one):
        lax.fori_loop(first, last, one, 0, unroll=min(12, last - first))

    def decode_q(first, last):
        def one(pos, _):
            i, hi, lo = decode(0, pos)
            at = pl.ds(pl.multiple_of(i * 48, 16), 48)
            kat = pl.ds(pl.multiple_of(i * 16, 16), 16)
            for h in range(2):
                qm[h, at, 0:128] = hi[48 * h:48 * h + 48]
                qm[h, at, 128:256] = lo[48 * h:48 * h + 48]
                km[h, kat, 0:128] = hi[96 + 16 * h:112 + 16 * h]
                km[h, kat, 128:256] = lo[96 + 16 * h:112 + 16 * h]
            return 0

        over(first, last, one)

    def fold_q(h):
        qf_ref[h] = fold(qm[h], km[h])

    def decode_o(h, first, last):
        om, vm = ((om0, vm0), (om1, vm1))[h]

        def one(pos, _):
            i, hi, lo = decode(1 + h, pos)
            at = pl.ds(pl.multiple_of(i * 112, 16), 112)
            vat = pl.ds(pl.multiple_of(i * 16, 16), 16)
            om[at, 0:128] = hi[:112]
            om[at, 128:256] = lo[:112]
            vm[vat, 0:128] = hi[112:]
            vm[vat, 128:256] = lo[112:]
            return 0

        over(first, last, one)

    def fold_o():
        def tile(i, _):
            at = pl.ds(pl.multiple_of(i * 256, 256), 256)
            of_ref[:, at] = fold(vm0[...], om0[at])
            return 0

        lax.fori_loop(0, EARLY, tile, 0, unroll=EARLY)

    order = (3, 0, 1, 2)
    for t in order:
        own(t)
    far_out(0)
    far_out(3)
    for t in order:
        forward(t, 0)
    for t in order:
        partner(t)
    far_out(1)
    far_out(2)
    maps()
    for t in order:
        forward(t, 1)
    far_in(0)
    own(4)
    far_in(3)
    own(7)
    for t in order:
        finish(t)
        near_out(t)
    far_in(1)
    own(5)
    forward(7, 0)
    forward(4, 0)
    partner(7)
    partner(4)
    far_in(2)
    own(6)
    forward(5, 0)
    cross(5)
    forward(7, 1)
    forward(4, 1)
    finish(7)
    near_in(3)
    scales()
    near_in(0)
    decode_q(0, NEAR)
    forward(6, 0)
    partner(6)
    near_in(1)
    decode_o(0, 0, NEAR)
    near_in(2)
    decode_o(1, 0, NEAR)
    cross_far(5)
    finish(4)
    decode_q(NEAR, ND)
    fold_q(0)
    fold_q(1)
    forward(6, 1)
    finish_cross(5)
    decode_o(0, NEAR, ND)
    fold_o()
    finish(6)
    decode_o(1, NEAR, ND)
    for c in started:
        c.wait_send()
    for t in range(4):
        sent = ssend if t == 3 else send.at[t]
        pltpu.make_async_copy(sent, sent, a_send.at[t]).wait()
        sent = (nsc if t == 3 else near.at[t]).at[:, pl.ds(0, NEAR - 1)]
        pltpu.make_async_copy(sent, sent, x_send.at[t]).wait()


def last_kernel(qf_ref, of_ref, om0, vm0, om1, vm1, q_out, o_out, held, sem):
    copies = [pltpu.make_async_copy(qf_ref, q_out, sem.at[0]),
              pltpu.make_async_copy(of_ref, o_out.at[0, :, pl.ds(0, 256 * EARLY)], sem.at[1])]
    for c in copies:
        c.start()
    for n in range(EARLY, 2 * TILES):
        h, i = n // TILES, n % TILES
        om, vm = ((om0, vm0), (om1, vm1))[h]
        at = pl.ds(256 * i, 256)
        held[h, :, at] = fold(vm[...], om[at])
        c = pltpu.make_async_copy(held.at[h, :, at], o_out.at[h, :, at], sem.at[2 + n])
        c.start()
        copies.append(c)
    for c in copies:
        c.wait()


def body(stored_q, stored_kv, stored_o, owner_map):
    vmem = pl.BlockSpec(memory_space=pltpu.VMEM)
    hbm = pl.BlockSpec(memory_space=pltpu.HBM)
    dma = pltpu.SemaphoreType.DMA
    far_inputs = [pltpu.with_memory_space_constraint(x, pltpu.HBM) for x in (
        stored_q.reshape(6, 64, 128),
        stored_kv.reshape(2, ND, 4, 128).transpose(1, 2, 0, 3).reshape(ND, 8, 128),
        stored_o.reshape(14, 64, 128),
        owner_map.T)]
    parts = pl.pallas_call(
        kernel,
        out_shape=(pltpu.VMEM((2, 1536, 512), BF16), pltpu.VMEM((512, 256 * EARLY), BF16),
                   pltpu.VMEM((3584, 256), BF16), pltpu.VMEM((512, 256), BF16),
                   pltpu.VMEM((3584, 256), BF16), pltpu.VMEM((512, 256), BF16)),
        in_specs=[hbm] * 4,
        out_specs=[vmem] * 6,
        scratch_shapes=[
            pltpu.VMEM((6, 64, 128), F32),
            pltpu.VMEM((ND, 8, 128), F32),
            pltpu.VMEM((14, 64, 128), F32),
            pltpu.VMEM((NG, ND), I32),
            pltpu.VMEM((3, NG, NEAR, ROWS, 128), jnp.int16),
            pltpu.VMEM((NG, NEAR, 1, 128), F32),
            pltpu.VMEM((3, FAR, ROWS, 128), jnp.int16),
            pltpu.VMEM((FAR, 1, 128), F32),
            pltpu.VMEM((3, NG, ND, ROWS, 128), jnp.int16),
            pltpu.VMEM((NG, ND, 1, 128), F32),
            pltpu.VMEM((3, ND, 128), F32),
            pltpu.VMEM((2, 128, 128), I32),
            pltpu.VMEM((ND, 128), I32),
            pltpu.VMEM((2, 1536, 256), BF16),
            pltpu.VMEM((2, 512, 256), BF16),
            dma((4,)), dma((4,)), dma((4,)), dma((4,)), dma((4,)), dma((72,)), dma((72,)),
        ],
        compiler_params=pltpu.CompilerParams(
            collective_id=0, has_side_effects=True, vmem_limit_bytes=32 * 1024 * 1024),
    )(*far_inputs)
    return pl.pallas_call(
        last_kernel,
        out_shape=(jax.ShapeDtypeStruct((2, 1536, 512), BF16), jax.ShapeDtypeStruct((2, 512, 3584), BF16)),
        in_specs=[vmem] * 6,
        out_specs=[hbm] * 2,
        scratch_shapes=[pltpu.VMEM((2, 512, 3584), BF16), dma((2 + 2 * TILES,))],
        compiler_params=pltpu.CompilerParams(vmem_limit_bytes=32 * 1024 * 1024),
    )(*parts)


def solution(mesh):
    in_specs = (P("group", "dev", None), P("group", "dev", None), P("group", "dev", None), P())
    out_specs = (P("dev", None, None), P("dev", None, None))
    return jax.shard_map(body, mesh=mesh, in_specs=in_specs, out_specs=out_specs, check_vma=False)
```

```python
import jax
import jax.numpy as jnp
from jax import lax
from jax.experimental import pallas as pl
from jax.experimental.pallas import tpu as pltpu
from jax.sharding import PartitionSpec as P

MESH = pl.DeviceIdType.MESH
F32, BF16, I32 = jnp.float32, jnp.bfloat16, jnp.int32
NG, ND = 8, 32
ROWS = 16
TILES, EARLY = 14, 7
NEAR, FAR = 8, 24
GROW = 1.008 / 32767.0
LEAST = 2.0**-120


def nt(a, b):
    return lax.dot_general(a, b, (((1,), (1,)), ((), ())), preferred_element_type=F32)


def fold(a, b):
    hi = b[:, 0:128]
    return (nt(a, jnp.concatenate([hi, hi], axis=1)) + nt(a[:, 0:128], b[:, 128:256])).astype(BF16)


def kernel(q_hbm, kv_hbm, o_hbm, own_hbm, qf_ref, of_ref, om0, vm0, om1, vm1,
           q_ref, kv_ref, o_ref, own_ref, near, nsc, send, ssend, gat, gsc, sca, jmap, inv, qm, km,
           in_sem, a_send, a_recv, x_send, x_recv, s_send, s_recv):
    loads = [pltpu.make_async_copy(a, b, in_sem.at[n])
             for n, (a, b) in enumerate(((q_hbm, q_ref), (kv_hbm, kv_ref), (o_hbm, o_ref), (own_hbm, own_ref)))]
    for c in loads:
        c.start()
    g = lax.axis_index("group")
    d = lax.axis_index("dev")
    zl, y = g // 4, g % 4
    zh, xc = (d // 2) % 4, (d // 8) * 2 + d % 2
    up, down, far = (y + 1) % 4, (y + 3) % 4, (y + 2) % 4
    mine, other = zl * 4, (1 - zl) * 4
    to_z, to_p, to_m = (other + y, d), (mine + up, d), (mine + down, d)

    def dev_at(z, n):
        return ((n // 2) * 4 + z) * 2 + n % 2

    barrier = pltpu.get_barrier_semaphore()

    def greet(i, _):
        who = dev_at((zh + 2 + i // NEAR) % 4, (xc + 4 + i) % NEAR)

        @pl.when(who != d)
        def _():
            pl.semaphore_signal(barrier, inc=1, device_id=(g, who), device_id_type=MESH)
        return 0

    lax.fori_loop(0, ND, greet, 0)
    for who in (to_z, to_p, to_m):
        pl.semaphore_signal(barrier, inc=1, device_id=who, device_id_type=MESH)

    row = lax.broadcasted_iota(I32, (ROWS, 128), 0)
    lane = lax.broadcasted_iota(I32, (ROWS, 128), 1)

    def quantise(i):
        qs = [q_ref[:, 2 * i + h, :] for h in range(2)]
        os = [o_ref[:, 2 * i + h, :] for h in range(2)]
        ks = [kv_ref[i, 2 * h:2 * h + 2, :] for h in range(4)]
        blocks = (
            jnp.concatenate([qs[0], qs[1], ks[0], ks[2]], axis=0),
            jnp.concatenate([os[0], ks[1]], axis=0),
            jnp.concatenate([os[1], ks[3]], axis=0),
        )
        codes, packed = [], jnp.zeros((1, 128), F32)
        for t, x in enumerate(blocks):
            top = jnp.max(jnp.abs(x), axis=1, keepdims=True)
            scale = jnp.maximum((top * GROW).astype(BF16).astype(F32), LEAST)
            codes.append(jnp.round(x * (1.0 / scale)).astype(I32).astype(jnp.int16))
            spread = jnp.where(lane == row + ROWS * ((t + g) % NG), scale, 0.0)
            packed = packed + jnp.sum(spread, axis=0, keepdims=True)
        return codes, packed

    def code_near(n, _):
        codes, packed = quantise(dev_at(zh, n))
        for t in range(3):
            near[t, g, n] = codes[t]
        nsc[g, n] = packed
        return 0

    def code_far(n, _):
        codes, packed = quantise(dev_at((zh + 1 + n // NEAR) % 4, n % NEAR))
        for t in range(3):
            send[t, n] = codes[t]
        ssend[n] = packed
        return 0

    for c in loads:
        c.wait()
    lax.fori_loop(0, FAR, code_far, 0, unroll=4)
    lax.fori_loop(0, NEAR, code_near, 0, unroll=4)
    pl.semaphore_wait(barrier, ND + 2)

    def into(part, group):
        if part < 4:
            return nsc.at[group] if part == 3 else near.at[part, group]
        ref = gsc.at[group] if part == 7 else gat.at[part - 4, group]
        return ref.at[pl.ds(NEAR, FAR)]

    def half(part, group, n):
        size = (NEAR if part < 4 else FAR) // 2
        return into(part, group).at[pl.ds(n * size, size)]

    def hop(part, kind, ref, who):
        n = part * 9 + kind
        return pltpu.make_async_remote_copy(
            src_ref=ref, dst_ref=ref, send_sem=s_send.at[n], recv_sem=s_recv.at[n],
            device_id=who, device_id_type=MESH)

    started = []

    def go(*args):
        c = hop(*args)
        c.start()
        started.append(c)

    def own(part):
        own_z(part)
        own_y(part)

    def own_z(part):
        go(part, 0, into(part, g), to_z)

    def own_y(part):
        go(part, 1, into(part, g), to_p)
        go(part, 2, into(part, g), to_m)

    def partner(part):
        ref = into(part, other + y)
        hop(part, 0, ref, to_z).wait_recv()
        go(part, 3, ref, to_p)
        go(part, 4, ref, to_m)

    def forward(part, b):
        base = (mine, other)[b]
        hop(part, 1 + 2 * b, into(part, base + down), to_p).wait_recv()
        go(part, 5 + 2 * b, half(part, base + down, 0), to_p)
        hop(part, 2 + 2 * b, into(part, base + up), to_m).wait_recv()
        go(part, 6 + 2 * b, half(part, base + up, 1), to_m)

    def finish(part):
        for b, base in enumerate((mine, other)):
            hop(part, 5 + 2 * b, half(part, base + far, 0), to_p).wait_recv()
            hop(part, 6 + 2 * b, half(part, base + far, 1), to_m).wait_recv()

    def cross(part):
        go(part, 3, into(part, mine + down), to_z)
        go(part, 4, into(part, mine + up), to_z)

    def cross_far(part):
        hop(part, 5, half(part, mine + far, 0), to_p).wait_recv()
        hop(part, 6, half(part, mine + far, 1), to_m).wait_recv()
        go(part, 7, into(part, mine + far), to_z)

    def finish_cross(part):
        for kind, group in ((0, y), (3, down), (4, up), (7, far)):
            hop(part, kind, into(part, other + group), to_z).wait_recv()

    def far_out(t):
        src = ssend if t == 3 else send.at[t]
        dst = gsc.at[g] if t == 3 else gat.at[t, g]

        def one(k, _):
            rel, n = k // NEAR, (xc + k) % NEAR
            pltpu.make_async_remote_copy(
                src_ref=src.at[rel * NEAR + n], dst_ref=dst.at[NEAR + (2 - rel) * NEAR + xc],
                send_sem=a_send.at[t], recv_sem=a_recv.at[t],
                device_id=(g, dev_at((zh + 1 + rel) % 4, n)), device_id_type=MESH).start()
            return 0

        lax.fori_loop(0, FAR, one, 0)

    def far_in(t):
        whole = into(t + 4, g)
        pltpu.make_async_copy(whole, whole, a_recv.at[t]).wait()

    def near_out(t):
        src = nsc if t == 3 else near.at[t]
        dst = gsc if t == 3 else gat.at[t]

        def one(k, _):
            n = (xc + k) % NEAR
            pltpu.make_async_remote_copy(
                src_ref=src.at[:, n], dst_ref=dst.at[:, xc],
                send_sem=x_send.at[t], recv_sem=x_recv.at[t],
                device_id=(g, dev_at(zh, n)), device_id_type=MESH).start()
            return 0

        lax.fori_loop(1, NEAR, one, 0)
        for n in range(NG):
            if t == 3:
                gsc[n, xc] = nsc[n, xc]
            else:
                gat[t, n, xc] = near[t, n, xc]

    def near_in(t):
        whole = (gsc if t == 3 else gat.at[t]).at[:, pl.ds(0, NEAR - 1)]
        pltpu.make_async_copy(whole, whole, x_recv.at[t]).wait()

    def maps():
        r = lax.broadcasted_iota(I32, (128, 128), 0)
        k = lax.broadcasted_iota(I32, (128, 128), 1)
        kin = k - (k // ROWS) * ROWS

        def piece(rem, size):
            return sum(((rem >= size * n).astype(I32) for n in range(1, NG)), jnp.zeros_like(rem))

        h1 = (r >= 48).astype(I32)
        rq = r - 48 * h1
        jq = piece(rq, 6)
        h2 = (r >= 112).astype(I32)
        rk = r - 96 - 16 * h2
        jk = piece(rk, 2)
        offset = jnp.where(r < 96, rq - 6 * jq + 6 * h1, rk - 2 * jk + 12 + 2 * h2)
        jmap[0] = jnp.where(offset == kin, jnp.where(r < 96, jq, jk), -1)
        jo = piece(r, 14)
        rv = r - 112
        jv = piece(rv, 2)
        offset = jnp.where(r < 112, r - 14 * jo, rv - 2 * jv + 14)
        jmap[1] = jnp.where(offset == kin, jnp.where(r < 112, jo, jv), -1)
        kg = lax.broadcasted_iota(I32, (ND, 128), 1) // ROWS
        held = jnp.zeros((ND, 128), I32)
        owner = own_ref[...].T
        for j in range(NG):
            held = held + jnp.where(owner[:, j:j + 1] == kg, j, 0)
        inv[...] = held

    def scales():
        at = lax.broadcasted_iota(I32, (ND, 128), 1) // ROWS
        lines = [gsc[n].reshape(ND, 128) for n in range(NG)]
        for t in range(3):
            held = jnp.zeros((ND, 128), F32)
            for n in range(NG):
                held = held + jnp.where(at == (n + t) % NG, lines[n], 0.0)
            sca[t] = pltpu.roll(held, (128 - ROWS * t) % 128, 1)

    def decode(t, pos):
        i = dev_at((zh + pos // NEAR) % 4, pos % NEAR)
        code = gat[t, :, pos].reshape(128, 128).astype(F32)
        hi = code.astype(BF16)
        lo = (code - hi.astype(F32)).astype(BF16)
        pick = jnp.where(jmap[min(t, 1)] == inv[pl.ds(i, 1), :], sca[t, pl.ds(pos, 1), :], 0.0).astype(BF16)
        x = jnp.dot(jnp.concatenate([pick, pick], axis=1), jnp.concatenate([hi, lo], axis=0),
                    preferred_element_type=F32)
        hi = x.astype(BF16)
        return i, hi, (x - hi.astype(F32)).astype(BF16)

    def over(first, last, one):
        lax.fori_loop(first, last, one, 0, unroll=min(12, last - first))

    def decode_q(first, last):
        def one(pos, _):
            i, hi, lo = decode(0, pos)
            at = pl.ds(pl.multiple_of(i * 48, 16), 48)
            kat = pl.ds(pl.multiple_of(i * 16, 16), 16)
            for h in range(2):
                qm[h, at, 0:128] = hi[48 * h:48 * h + 48]
                qm[h, at, 128:256] = lo[48 * h:48 * h + 48]
                km[h, kat, 0:128] = hi[96 + 16 * h:112 + 16 * h]
                km[h, kat, 128:256] = lo[96 + 16 * h:112 + 16 * h]
            return 0

        over(first, last, one)

    def fold_q(h):
        qf_ref[h] = fold(qm[h], km[h])

    def decode_o(h, first, last):
        om, vm = ((om0, vm0), (om1, vm1))[h]

        def one(pos, _):
            i, hi, lo = decode(1 + h, pos)
            at = pl.ds(pl.multiple_of(i * 112, 16), 112)
            vat = pl.ds(pl.multiple_of(i * 16, 16), 16)
            om[at, 0:128] = hi[:112]
            om[at, 128:256] = lo[:112]
            vm[vat, 0:128] = hi[112:]
            vm[vat, 128:256] = lo[112:]
            return 0

        over(first, last, one)

    def fold_o():
        def tile(i, _):
            at = pl.ds(pl.multiple_of(i * 256, 256), 256)
            of_ref[:, at] = fold(vm0[...], om0[at])
            return 0

        lax.fori_loop(0, EARLY, tile, 0, unroll=EARLY)

    order = (3, 0, 1, 2)
    for t in order:
        own(t)
    far_out(0)
    far_out(3)
    for t in order:
        forward(t, 0)
    for t in order:
        partner(t)
    far_out(1)
    far_out(2)
    maps()
    for t in order:
        forward(t, 1)
    far_in(0)
    own(4)
    far_in(3)
    own(7)
    for t in order:
        finish(t)
        near_out(t)
    far_in(1)
    own(5)
    forward(7, 0)
    forward(4, 0)
    partner(7)
    partner(4)
    far_in(2)
    own(6)
    forward(5, 0)
    cross(5)
    forward(7, 1)
    forward(4, 1)
    partner(6)
    finish(7)
    near_in(3)
    scales()
    near_in(0)
    decode_q(0, NEAR)
    forward(6, 0)
    near_in(1)
    decode_o(0, 0, NEAR)
    near_in(2)
    decode_o(1, 0, NEAR)
    cross_far(5)
    finish(4)
    decode_q(NEAR, ND)
    fold_q(0)
    fold_q(1)
    forward(6, 1)
    finish_cross(5)
    decode_o(0, NEAR, ND)
    fold_o()
    finish(6)
    decode_o(1, NEAR, ND)
    for c in started:
        c.wait_send()
    for t in range(4):
        sent = ssend if t == 3 else send.at[t]
        pltpu.make_async_copy(sent, sent, a_send.at[t]).wait()
        sent = (nsc if t == 3 else near.at[t]).at[:, pl.ds(0, NEAR - 1)]
        pltpu.make_async_copy(sent, sent, x_send.at[t]).wait()


def last_kernel(qf_ref, of_ref, om0, vm0, om1, vm1, q_out, o_out, held, sem):
    copies = [pltpu.make_async_copy(qf_ref, q_out, sem.at[0]),
              pltpu.make_async_copy(of_ref, o_out.at[0, :, pl.ds(0, 256 * EARLY)], sem.at[1])]
    for c in copies:
        c.start()
    for n in range(EARLY, 2 * TILES):
        h, i = n // TILES, n % TILES
        om, vm = ((om0, vm0), (om1, vm1))[h]
        at = pl.ds(256 * i, 256)
        held[h, :, at] = fold(vm[...], om[at])
        c = pltpu.make_async_copy(held.at[h, :, at], o_out.at[h, :, at], sem.at[2 + n])
        c.start()
        copies.append(c)
    for c in copies:
        c.wait()


def body(stored_q, stored_kv, stored_o, owner_map):
    vmem = pl.BlockSpec(memory_space=pltpu.VMEM)
    hbm = pl.BlockSpec(memory_space=pltpu.HBM)
    dma = pltpu.SemaphoreType.DMA
    far_inputs = [pltpu.with_memory_space_constraint(x, pltpu.HBM) for x in (
        stored_q.reshape(6, 64, 128),
        stored_kv.reshape(2, ND, 4, 128).transpose(1, 2, 0, 3).reshape(ND, 8, 128),
        stored_o.reshape(14, 64, 128),
        owner_map.T)]
    parts = pl.pallas_call(
        kernel,
        out_shape=(pltpu.VMEM((2, 1536, 512), BF16), pltpu.VMEM((512, 256 * EARLY), BF16),
                   pltpu.VMEM((3584, 256), BF16), pltpu.VMEM((512, 256), BF16),
                   pltpu.VMEM((3584, 256), BF16), pltpu.VMEM((512, 256), BF16)),
        in_specs=[hbm] * 4,
        out_specs=[vmem] * 6,
        scratch_shapes=[
            pltpu.VMEM((6, 64, 128), F32),
            pltpu.VMEM((ND, 8, 128), F32),
            pltpu.VMEM((14, 64, 128), F32),
            pltpu.VMEM((NG, ND), I32),
            pltpu.VMEM((3, NG, NEAR, ROWS, 128), jnp.int16),
            pltpu.VMEM((NG, NEAR, 1, 128), F32),
            pltpu.VMEM((3, FAR, ROWS, 128), jnp.int16),
            pltpu.VMEM((FAR, 1, 128), F32),
            pltpu.VMEM((3, NG, ND, ROWS, 128), jnp.int16),
            pltpu.VMEM((NG, ND, 1, 128), F32),
            pltpu.VMEM((3, ND, 128), F32),
            pltpu.VMEM((2, 128, 128), I32),
            pltpu.VMEM((ND, 128), I32),
            pltpu.VMEM((2, 1536, 256), BF16),
            pltpu.VMEM((2, 512, 256), BF16),
            dma((4,)), dma((4,)), dma((4,)), dma((4,)), dma((4,)), dma((72,)), dma((72,)),
        ],
        compiler_params=pltpu.CompilerParams(
            collective_id=0, has_side_effects=True, vmem_limit_bytes=32 * 1024 * 1024),
    )(*far_inputs)
    return pl.pallas_call(
        last_kernel,
        out_shape=(jax.ShapeDtypeStruct((2, 1536, 512), BF16), jax.ShapeDtypeStruct((2, 512, 3584), BF16)),
        in_specs=[vmem] * 6,
        out_specs=[hbm] * 2,
        scratch_shapes=[pltpu.VMEM((2, 512, 3584), BF16), dma((2 + 2 * TILES,))],
        compiler_params=pltpu.CompilerParams(vmem_limit_bytes=32 * 1024 * 1024),
    )(*parts)


def solution(mesh):
    in_specs = (P("group", "dev", None), P("group", "dev", None), P("group", "dev", None), P())
    out_specs = (P("dev", None, None), P("dev", None, None))
    return jax.shard_map(body, mesh=mesh, in_specs=in_specs, out_specs=out_specs, check_vma=False)
```

```python
import jax
import jax.numpy as jnp
from jax import lax
from jax.experimental import pallas as pl
from jax.experimental.pallas import tpu as pltpu
from jax.sharding import PartitionSpec as P

MESH = pl.DeviceIdType.MESH
F32, BF16, I32 = jnp.float32, jnp.bfloat16, jnp.int32
NG, ND = 8, 32
ROWS = 16
TILES, EARLY = 14, 7
NEAR, FAR = 8, 24
GROW = 1.008 / 32767.0
LEAST = 2.0**-120


def nt(a, b):
    return lax.dot_general(a, b, (((1,), (1,)), ((), ())), preferred_element_type=F32)


def fold(a, b):
    hi = b[:, 0:128]
    return (nt(a, jnp.concatenate([hi, hi], axis=1)) + nt(a[:, 0:128], b[:, 128:256])).astype(BF16)


def kernel(q_hbm, kv_hbm, o_hbm, own_hbm, qf_ref, of_ref, om0, vm0, om1, vm1,
           q_ref, kv_ref, o_ref, own_ref, near, nsc, send, ssend, gat, gsc, sca, jmap, inv, qm, km,
           in_sem, a_send, a_recv, x_send, x_recv, s_send, s_recv):
    loads = [pltpu.make_async_copy(a, b, in_sem.at[n])
             for n, (a, b) in enumerate(((q_hbm, q_ref), (kv_hbm, kv_ref), (o_hbm, o_ref), (own_hbm, own_ref)))]
    for c in loads:
        c.start()
    g = lax.axis_index("group")
    d = lax.axis_index("dev")
    zl, y = g // 4, g % 4
    zh, xc = (d // 2) % 4, (d // 8) * 2 + d % 2
    up, down, far = (y + 1) % 4, (y + 3) % 4, (y + 2) % 4
    mine, other = zl * 4, (1 - zl) * 4
    to_z, to_p, to_m = (other + y, d), (mine + up, d), (mine + down, d)

    def dev_at(z, n):
        return ((n // 2) * 4 + z) * 2 + n % 2

    barrier = pltpu.get_barrier_semaphore()

    def greet(i, _):
        who = dev_at((zh + 2 + i // NEAR) % 4, (xc + 4 + i) % NEAR)

        @pl.when(who != d)
        def _():
            pl.semaphore_signal(barrier, inc=1, device_id=(g, who), device_id_type=MESH)
        return 0

    lax.fori_loop(0, ND, greet, 0)
    for who in (to_z, to_p, to_m):
        pl.semaphore_signal(barrier, inc=1, device_id=who, device_id_type=MESH)

    row = lax.broadcasted_iota(I32, (ROWS, 128), 0)
    lane = lax.broadcasted_iota(I32, (ROWS, 128), 1)

    def quantise(i):
        qs = [q_ref[:, 2 * i + h, :] for h in range(2)]
        os = [o_ref[:, 2 * i + h, :] for h in range(2)]
        ks = [kv_ref[i, 2 * h:2 * h + 2, :] for h in range(4)]
        blocks = (
            jnp.concatenate([qs[0], qs[1], ks[0], ks[2]], axis=0),
            jnp.concatenate([os[0], ks[1]], axis=0),
            jnp.concatenate([os[1], ks[3]], axis=0),
        )
        codes, packed = [], jnp.zeros((1, 128), F32)
        for t, x in enumerate(blocks):
            top = jnp.max(jnp.abs(x), axis=1, keepdims=True)
            scale = jnp.maximum((top * GROW).astype(BF16).astype(F32), LEAST)
            codes.append(jnp.round(x * (1.0 / scale)).astype(I32).astype(jnp.int16))
            spread = jnp.where(lane == row + ROWS * ((t + g) % NG), scale, 0.0)
            packed = packed + jnp.sum(spread, axis=0, keepdims=True)
        return codes, packed

    def code_near(n, _):
        codes, packed = quantise(dev_at(zh, n))
        for t in range(3):
            near[t, g, n] = codes[t]
        nsc[g, n] = packed
        return 0

    def code_far(n, _):
        codes, packed = quantise(dev_at((zh + 1 + n // NEAR) % 4, n % NEAR))
        for t in range(3):
            send[t, n] = codes[t]
        ssend[n] = packed
        return 0

    for c in loads:
        c.wait()
    lax.fori_loop(0, FAR, code_far, 0, unroll=4)
    lax.fori_loop(0, NEAR, code_near, 0, unroll=4)
    pl.semaphore_wait(barrier, ND + 2)

    def into(part, group):
        if part < 4:
            return nsc.at[group] if part == 3 else near.at[part, group]
        ref = gsc.at[group] if part == 7 else gat.at[part - 4, group]
        return ref.at[pl.ds(NEAR, FAR)]

    def half(part, group, n):
        size = (NEAR if part < 4 else FAR) // 2
        return into(part, group).at[pl.ds(n * size, size)]

    def hop(part, kind, ref, who):
        n = part * 9 + kind
        return pltpu.make_async_remote_copy(
            src_ref=ref, dst_ref=ref, send_sem=s_send.at[n], recv_sem=s_recv.at[n],
            device_id=who, device_id_type=MESH)

    started = []

    def go(*args):
        c = hop(*args)
        c.start()
        started.append(c)

    def own(part):
        own_z(part)
        own_y(part)

    def own_z(part):
        go(part, 0, into(part, g), to_z)

    def own_y(part):
        go(part, 1, into(part, g), to_p)
        go(part, 2, into(part, g), to_m)

    def partner(part):
        ref = into(part, other + y)
        hop(part, 0, ref, to_z).wait_recv()
        go(part, 3, ref, to_p)
        go(part, 4, ref, to_m)

    def forward(part, b):
        base = (mine, other)[b]
        hop(part, 1 + 2 * b, into(part, base + down), to_p).wait_recv()
        go(part, 5 + 2 * b, half(part, base + down, 0), to_p)
        hop(part, 2 + 2 * b, into(part, base + up), to_m).wait_recv()
        go(part, 6 + 2 * b, half(part, base + up, 1), to_m)

    def finish_half(part, n):
        for b, base in enumerate((mine, other)):
            hop(part, 5 + 2 * b + n, half(part, base + far, n), (to_p, to_m)[n]).wait_recv()

    def finish(part):
        for n in range(2):
            finish_half(part, n)

    def cross(part):
        go(part, 3, into(part, mine + down), to_z)
        go(part, 4, into(part, mine + up), to_z)

    def cross_far(part):
        hop(part, 5, half(part, mine + far, 0), to_p).wait_recv()
        hop(part, 6, half(part, mine + far, 1), to_m).wait_recv()
        go(part, 7, into(part, mine + far), to_z)

    def finish_cross(part):
        for kind, group in ((0, y), (3, down), (4, up), (7, far)):
            hop(part, kind, into(part, other + group), to_z).wait_recv()

    def far_out(t):
        src = ssend if t == 3 else send.at[t]
        dst = gsc.at[g] if t == 3 else gat.at[t, g]

        def one(k, _):
            rel, n = k // NEAR, (xc + k) % NEAR
            pltpu.make_async_remote_copy(
                src_ref=src.at[rel * NEAR + n], dst_ref=dst.at[NEAR + (2 - rel) * NEAR + xc],
                send_sem=a_send.at[t], recv_sem=a_recv.at[t],
                device_id=(g, dev_at((zh + 1 + rel) % 4, n)), device_id_type=MESH).start()
            return 0

        lax.fori_loop(0, FAR, one, 0)

    def far_in(t):
        whole = into(t + 4, g)
        pltpu.make_async_copy(whole, whole, a_recv.at[t]).wait()

    def near_out(t):
        src = nsc if t == 3 else near.at[t]
        dst = gsc if t == 3 else gat.at[t]

        def one(k, _):
            n = (xc + k) % NEAR
            pltpu.make_async_remote_copy(
                src_ref=src.at[:, n], dst_ref=dst.at[:, xc],
                send_sem=x_send.at[t], recv_sem=x_recv.at[t],
                device_id=(g, dev_at(zh, n)), device_id_type=MESH).start()
            return 0

        lax.fori_loop(1, NEAR, one, 0)
        for n in range(NG):
            if t == 3:
                gsc[n, xc] = nsc[n, xc]
            else:
                gat[t, n, xc] = near[t, n, xc]

    def near_in(t):
        whole = (gsc if t == 3 else gat.at[t]).at[:, pl.ds(0, NEAR - 1)]
        pltpu.make_async_copy(whole, whole, x_recv.at[t]).wait()

    def maps():
        r = lax.broadcasted_iota(I32, (128, 128), 0)
        k = lax.broadcasted_iota(I32, (128, 128), 1)
        kin = k - (k // ROWS) * ROWS

        def piece(rem, size):
            return sum(((rem >= size * n).astype(I32) for n in range(1, NG)), jnp.zeros_like(rem))

        h1 = (r >= 48).astype(I32)
        rq = r - 48 * h1
        jq = piece(rq, 6)
        h2 = (r >= 112).astype(I32)
        rk = r - 96 - 16 * h2
        jk = piece(rk, 2)
        offset = jnp.where(r < 96, rq - 6 * jq + 6 * h1, rk - 2 * jk + 12 + 2 * h2)
        jmap[0] = jnp.where(offset == kin, jnp.where(r < 96, jq, jk), -1)
        jo = piece(r, 14)
        rv = r - 112
        jv = piece(rv, 2)
        offset = jnp.where(r < 112, r - 14 * jo, rv - 2 * jv + 14)
        jmap[1] = jnp.where(offset == kin, jnp.where(r < 112, jo, jv), -1)
        kg = lax.broadcasted_iota(I32, (ND, 128), 1) // ROWS
        held = jnp.zeros((ND, 128), I32)
        owner = own_ref[...].T
        for j in range(NG):
            held = held + jnp.where(owner[:, j:j + 1] == kg, j, 0)
        inv[...] = held

    def scales():
        at = lax.broadcasted_iota(I32, (ND, 128), 1) // ROWS
        lines = [gsc[n].reshape(ND, 128) for n in range(NG)]
        for t in range(3):
            held = jnp.zeros((ND, 128), F32)
            for n in range(NG):
                held = held + jnp.where(at == (n + t) % NG, lines[n], 0.0)
            sca[t] = pltpu.roll(held, (128 - ROWS * t) % 128, 1)

    def decode(t, pos):
        i = dev_at((zh + pos // NEAR) % 4, pos % NEAR)
        code = gat[t, :, pos].reshape(128, 128).astype(F32)
        hi = code.astype(BF16)
        lo = (code - hi.astype(F32)).astype(BF16)
        pick = jnp.where(jmap[min(t, 1)] == inv[pl.ds(i, 1), :], sca[t, pl.ds(pos, 1), :], 0.0).astype(BF16)
        x = jnp.dot(jnp.concatenate([pick, pick], axis=1), jnp.concatenate([hi, lo], axis=0),
                    preferred_element_type=F32)
        hi = x.astype(BF16)
        return i, hi, (x - hi.astype(F32)).astype(BF16)

    def over(first, last, one):
        lax.fori_loop(first, last, one, 0, unroll=min(12, last - first))

    def decode_q(first, last):
        def one(pos, _):
            i, hi, lo = decode(0, pos)
            at = pl.ds(pl.multiple_of(i * 48, 16), 48)
            kat = pl.ds(pl.multiple_of(i * 16, 16), 16)
            for h in range(2):
                qm[h, at, 0:128] = hi[48 * h:48 * h + 48]
                qm[h, at, 128:256] = lo[48 * h:48 * h + 48]
                km[h, kat, 0:128] = hi[96 + 16 * h:112 + 16 * h]
                km[h, kat, 128:256] = lo[96 + 16 * h:112 + 16 * h]
            return 0

        over(first, last, one)

    def fold_q(h):
        qf_ref[h] = fold(qm[h], km[h])

    def decode_o(h, first, last):
        om, vm = ((om0, vm0), (om1, vm1))[h]

        def one(pos, _):
            i, hi, lo = decode(1 + h, pos)
            at = pl.ds(pl.multiple_of(i * 112, 16), 112)
            vat = pl.ds(pl.multiple_of(i * 16, 16), 16)
            om[at, 0:128] = hi[:112]
            om[at, 128:256] = lo[:112]
            vm[vat, 0:128] = hi[112:]
            vm[vat, 128:256] = lo[112:]
            return 0

        over(first, last, one)

    def fold_o():
        def tile(i, _):
            at = pl.ds(pl.multiple_of(i * 256, 256), 256)
            of_ref[:, at] = fold(vm0[...], om0[at])
            return 0

        lax.fori_loop(0, EARLY, tile, 0, unroll=EARLY)

    order = (3, 0, 1, 2)
    for t in order:
        own(t)
    far_out(0)
    far_out(3)
    for t in order:
        forward(t, 0)
    for t in order:
        partner(t)
    far_out(1)
    far_out(2)
    maps()
    for t in order:
        forward(t, 1)
    far_in(0)
    own(4)
    far_in(3)
    own(7)
    for t in order:
        finish(t)
        near_out(t)
    far_in(1)
    own(5)
    forward(7, 0)
    forward(4, 0)
    partner(7)
    partner(4)
    far_in(2)
    own(6)
    forward(5, 0)
    cross(5)
    forward(7, 1)
    forward(4, 1)
    partner(6)
    finish(7)
    near_in(3)
    scales()
    near_in(0)
    decode_q(0, NEAR)
    forward(6, 0)
    near_in(1)
    decode_o(0, 0, NEAR)
    near_in(2)
    decode_o(1, 0, NEAR)
    cross_far(5)
    finish(4)
    decode_q(NEAR, ND)
    fold_q(0)
    forward(6, 1)
    fold_q(1)
    finish_cross(5)
    decode_o(0, NEAR, ND)
    fold_o()
    for n in range(2):
        finish_half(6, n)
        decode_o(1, NEAR + n * FAR // 2, NEAR + (n + 1) * FAR // 2)
    for c in started:
        c.wait_send()
    for t in range(4):
        sent = ssend if t == 3 else send.at[t]
        pltpu.make_async_copy(sent, sent, a_send.at[t]).wait()
        sent = (nsc if t == 3 else near.at[t]).at[:, pl.ds(0, NEAR - 1)]
        pltpu.make_async_copy(sent, sent, x_send.at[t]).wait()


def last_kernel(qf_ref, of_ref, om0, vm0, om1, vm1, q_out, o_out, held, sem):
    copies = [pltpu.make_async_copy(qf_ref, q_out, sem.at[0]),
              pltpu.make_async_copy(of_ref, o_out.at[0, :, pl.ds(0, 256 * EARLY)], sem.at[1])]
    for c in copies:
        c.start()
    for n in range(EARLY, 2 * TILES):
        h, i = n // TILES, n % TILES
        om, vm = ((om0, vm0), (om1, vm1))[h]
        at = pl.ds(256 * i, 256)
        held[h, :, at] = fold(vm[...], om[at])
        c = pltpu.make_async_copy(held.at[h, :, at], o_out.at[h, :, at], sem.at[2 + n])
        c.start()
        copies.append(c)
    for c in copies:
        c.wait()


def body(stored_q, stored_kv, stored_o, owner_map):
    vmem = pl.BlockSpec(memory_space=pltpu.VMEM)
    hbm = pl.BlockSpec(memory_space=pltpu.HBM)
    dma = pltpu.SemaphoreType.DMA
    far_inputs = [pltpu.with_memory_space_constraint(x, pltpu.HBM) for x in (
        stored_q.reshape(6, 64, 128),
        stored_kv.reshape(2, ND, 4, 128).transpose(1, 2, 0, 3).reshape(ND, 8, 128),
        stored_o.reshape(14, 64, 128),
        owner_map.T)]
    parts = pl.pallas_call(
        kernel,
        out_shape=(pltpu.VMEM((2, 1536, 512), BF16), pltpu.VMEM((512, 256 * EARLY), BF16),
                   pltpu.VMEM((3584, 256), BF16), pltpu.VMEM((512, 256), BF16),
                   pltpu.VMEM((3584, 256), BF16), pltpu.VMEM((512, 256), BF16)),
        in_specs=[hbm] * 4,
        out_specs=[vmem] * 6,
        scratch_shapes=[
            pltpu.VMEM((6, 64, 128), F32),
            pltpu.VMEM((ND, 8, 128), F32),
            pltpu.VMEM((14, 64, 128), F32),
            pltpu.VMEM((NG, ND), I32),
            pltpu.VMEM((3, NG, NEAR, ROWS, 128), jnp.int16),
            pltpu.VMEM((NG, NEAR, 1, 128), F32),
            pltpu.VMEM((3, FAR, ROWS, 128), jnp.int16),
            pltpu.VMEM((FAR, 1, 128), F32),
            pltpu.VMEM((3, NG, ND, ROWS, 128), jnp.int16),
            pltpu.VMEM((NG, ND, 1, 128), F32),
            pltpu.VMEM((3, ND, 128), F32),
            pltpu.VMEM((2, 128, 128), I32),
            pltpu.VMEM((ND, 128), I32),
            pltpu.VMEM((2, 1536, 256), BF16),
            pltpu.VMEM((2, 512, 256), BF16),
            dma((4,)), dma((4,)), dma((4,)), dma((4,)), dma((4,)), dma((72,)), dma((72,)),
        ],
        compiler_params=pltpu.CompilerParams(
            collective_id=0, has_side_effects=True, vmem_limit_bytes=32 * 1024 * 1024),
    )(*far_inputs)
    return pl.pallas_call(
        last_kernel,
        out_shape=(jax.ShapeDtypeStruct((2, 1536, 512), BF16), jax.ShapeDtypeStruct((2, 512, 3584), BF16)),
        in_specs=[vmem] * 6,
        out_specs=[hbm] * 2,
        scratch_shapes=[pltpu.VMEM((2, 512, 3584), BF16), dma((2 + 2 * TILES,))],
        compiler_params=pltpu.CompilerParams(vmem_limit_bytes=32 * 1024 * 1024),
    )(*parts)


def solution(mesh):
    in_specs = (P("group", "dev", None), P("group", "dev", None), P("group", "dev", None), P())
    out_specs = (P("dev", None, None), P("dev", None, None))
    return jax.shard_map(body, mesh=mesh, in_specs=in_specs, out_specs=out_specs, check_vma=False)
```
